32 devices in a mesh: grp: 2 (over y), frm: 4 (over z), row: 4 (over x, core).
Axes of the slice: x: 2, y: 2, z: 4, core: 2. Of those that a mesh axis runs over, the one named last changes fastest.
Arguments:
- queries: bfloat16 [16, 8, 128, 2240], P(('grp', 'frm'), 'row'), parts along dimension 0, may hold values from -6 to 6
- keys: bfloat16 [16, 8, 128, 2240], P(('grp', 'frm'), 'row'), parts along dimension 0, may hold values from -6 to 6
- values: bfloat16 [16, 8, 128, 2240], P(('grp', 'frm'), 'row'), parts along dimension 0, may hold values from -6 to 6
- flags: int32 [16], P(('grp', 'frm')), parts along dimension 0, may hold values 0 or 1
- blocks: int32 [16], P(('grp', 'frm')), parts along dimension 0, may hold values from 0 to 2, as said below
- out_weight: bfloat16 [2240, 2240], P('frm'), may hold values from -0.125 to 0.125
- norm_gain: float32 [2240], replicated, may hold values from 0.1 to 1.9
Outputs:
- projected: bfloat16 [16, 8, 128, 2240], P(('grp', 'frm'), 'row'), parts along dimension 0
The draws below stay inside these ranges and needn't reach their ends.
There are 2 independent parts, one for each index of `grp`. The reference program is written for one: setup_inputs(seed, part) draws one part's arguments, and reference() takes and returns one part's arrays. A program takes and returns all parts, laid end to end along the dimension named above; an argument that names none is the same for every part. Nothing has to cross between parts.
Inputs may be any that keep to these rules, and one draw needn't show every extreme that they name: `flags`: 1 marks a clean frame, 0 a noisy one. `blocks`: within the 8 frames of one group, block numbers never fall and each block is 1 to 4 consecutive frames, some block exactly 4; every number from 0 to 2 occurs.
All inputs are finite; a program needn't handle non-finite values. No bound on the sum of `flags` on one device may be relied on, other than what follows from the above.
Results may differ from the reference program's by a relative error of at most 0.0049.
Values may be sent and summed in bfloat16 or wider, within the bound.
A program may use at most 192 MiB of HBM per device.

```python
import jax
import jax.numpy as jnp
from jax import lax

HEADS = 20
HD = 112
D = 2240
WL = 128
FRAMES = 8
HL = 8
BLOCKS = 3


def draw_blocks(key, part):
    base_key = jax.random.fold_in(key, 7301)
    first_key, loop_key = jax.random.split(base_key)
    chosen = jax.random.randint(first_key, (), 0, BLOCKS)
    positions = jnp.arange(BLOCKS, dtype=jnp.int32)
    lengths = jnp.ones((BLOCKS,), jnp.int32) + 3 * (positions == chosen).astype(jnp.int32)
    remain = FRAMES - BLOCKS - 3

    def place_one(step, current):
        step_key = jax.random.fold_in(loop_key, step)
        priority = jax.random.permutation(step_key, BLOCKS).astype(jnp.int32)
        scores = jnp.where(current < 4, priority, -1)
        target = jnp.argmax(scores)
        return current + (positions == target).astype(jnp.int32)
    lengths = lax.fori_loop(0, remain, place_one, lengths)
    ends = jnp.cumsum(lengths).astype(jnp.int32)
    frame_pos = jnp.arange(FRAMES, dtype=jnp.int32)
    return jnp.sum((ends[None, :] <= frame_pos[:, None]).astype(jnp.int32), axis=1).astype(jnp.int32)


def set_ends(values, key, smallest, largest):
    dims = values.shape
    index_at = [jax.random.randint(jax.random.fold_in(key, axis), (), 0, dims[axis]) for axis in range(len(dims))]
    values = values.at[tuple(index_at)].set(smallest)
    longest = dims.index(max(dims))
    index_at[longest] = (index_at[longest] + 1) % dims[longest]
    return values.at[tuple(index_at)].set(largest)


def block_scale(key, extent, cuts, smallest, largest):
    level, own = 1.0, jax.random.fold_in(key, 6)
    for axis_at, parts in cuts:
        steps = jnp.exp(jax.random.uniform(jax.random.fold_in(own, axis_at), (parts,), jnp.float32, smallest / len(cuts), largest / len(cuts)))
        level = level * jnp.repeat(steps, extent[axis_at] // parts).reshape([-1 if axis == axis_at else 1 for axis in range(len(extent))])
    return level


def bell_draw(rng, extent, deviation, most, shards=(), kind=jnp.bfloat16):
    factor_of = block_scale(rng, extent, shards, -0.22, 0.18) if shards else 1.0
    drawn = jax.random.normal(rng, extent, jnp.float32) * deviation * factor_of
    return jnp.minimum(jnp.maximum(drawn, -most), most).astype(kind)


def setup_inputs(seed: int = 0, part: int = 0) -> dict:
    seeds = jax.random.split(jax.random.key(seed), 8)
    part_splits = jax.random.split(jax.random.fold_in(seeds[7], part), 8)
    queries = bell_draw(part_splits[0], (FRAMES, HL, WL, D), 1.0, 6.0, ((0, 4), (1, 4)))
    keys = bell_draw(part_splits[1], (FRAMES, HL, WL, D), 1.0, 6.0, ((0, 4), (1, 4)))
    values = bell_draw(part_splits[2], (FRAMES, HL, WL, D), 1.0, 6.0, ((0, 4), (1, 4)))
    flags = set_ends((jax.random.randint(part_splits[3], (FRAMES,), 0, 2) < 1).astype(jnp.int32), jax.random.fold_in(part_splits[3], 1), 0, 1)
    blocks = draw_blocks(jax.random.fold_in(jax.random.fold_in(seeds[7], part), 71), part)
    out_weight = bell_draw(seeds[5], (D, D), D ** -0.5, 0.125, ((0, 4),))
    norm_gain = jnp.clip(1.0 + 0.18 * jax.random.normal(seeds[6], (D,), jnp.float32), 0.1, 1.9)
    return dict(queries=queries, keys=keys, values=values, flags=flags, blocks=blocks, out_weight=out_weight, norm_gain=norm_gain)


norm_eps = 1e-06

def reference(queries, keys, values, flags, blocks, out_weight, norm_gain):
    frames, lat_rows, lat_cols, model_width = queries.shape
    tokens = lat_rows * lat_cols
    weight_full = out_weight.astype(jnp.float32)
    gain_table = norm_gain.astype(jnp.float32).reshape(HEADS, HD)

    def frame_step(carried, inputs):
        closed, opened, latest = carried
        query_frame, key_frame, value_frame, flag_frame, block_frame = inputs
        key_pos = jax.nn.relu(key_frame).reshape(tokens, HEADS, HD).astype(jnp.float32)
        value_heads = value_frame.reshape(tokens, HEADS, HD).astype(jnp.float32)
        frame_state = jnp.einsum('tha,thb->hab', key_pos, value_heads, precision=lax.Precision.HIGHEST)
        flag_value = flag_frame.astype(jnp.float32)
        block_value = block_frame.astype(jnp.float32)
        advance = (latest < block_value).astype(jnp.float32)
        select = jnp.maximum(advance, flag_value)
        read_state = closed + select * opened + frame_state
        query_pos = jax.nn.relu(query_frame).reshape(tokens, HEADS, HD).astype(jnp.float32)
        attended = jnp.einsum('tha,hab->thb', query_pos, read_state, precision=lax.Precision.HIGHEST)
        inv_rms = lax.rsqrt(lax.optimization_barrier(jnp.mean(attended * attended, axis=-1, keepdims=True)) + norm_eps)
        normed = (attended * inv_rms * gain_table).astype(jnp.bfloat16).reshape(tokens, model_width)
        projected = jnp.dot(normed.astype(jnp.float32), weight_full, precision=lax.Precision.HIGHEST)
        projected = projected.astype(jnp.bfloat16).reshape(lat_rows, lat_cols, model_width)
        new_carry = (closed + advance * opened, flag_value * frame_state + (1.0 - advance) * opened, jnp.maximum(latest, block_value))
        return (new_carry, projected)
    initial = (jnp.zeros((HEADS, HD, HD), jnp.float32), jnp.zeros((HEADS, HD, HD), jnp.float32), jnp.array(-1.0, jnp.float32))
    _, outputs = lax.scan(frame_step, initial, (queries, keys, values, flags, blocks))
    return outputs
```

```python
import functools

import jax
import jax.numpy as jnp
from jax import lax
from jax.sharding import PartitionSpec as P
from jax.experimental import pallas as pl
from jax.experimental.pallas import tpu as pltpu

HEADS = 20
HD = 112


norm_eps = 1e-06


def entering(part, axis, combine, identity):
    place = lax.axis_index(axis)
    gathered = jax.tree.map(lambda a: lax.all_gather(a, axis), part)
    state = jax.tree.map(lambda a, e: jnp.zeros_like(a) + jnp.asarray(e, a.dtype), part, identity)

    def one(step, state):
        return combine(
            state, jax.tree.map(lambda a: lax.dynamic_index_in_dim(a, step, 0, False), gathered)
        )

    return lax.fori_loop(0, place, one, state)


def combine(earlier, later):
    closed_a, opened_a, latest_a = earlier
    closed_b, opened_b, latest_b = later
    advance = (latest_a < latest_b).astype(jnp.float32)
    return (
        closed_a + closed_b + advance * opened_a,
        opened_b + (1.0 - advance) * opened_a,
        jnp.maximum(latest_a, latest_b),
    )


def empty_carry(length):
    return (
        jnp.zeros((length,), jnp.float32),
        jnp.zeros((length,), jnp.float32),
        jnp.full((1,), -1.0, jnp.float32),
    )


def frame_element(frame_states, flag_values, block_values, frame_idx):
    length = frame_states.shape[1]
    return (
        jnp.zeros((length,), jnp.float32),
        flag_values[frame_idx] * frame_states[frame_idx],
        block_values[frame_idx : frame_idx + 1],
    )


def fold_frames(frame_states, flag_values, block_values):
    running = empty_carry(frame_states.shape[1])
    for frame_idx in range(frame_states.shape[0]):
        running = combine(
            running, frame_element(frame_states, flag_values, block_values, frame_idx)
        )
    return running


def read_frames(prefix, frame_states, flag_values, block_values):
    running = prefix
    collected = []
    for frame_idx in range(frame_states.shape[0]):
        advance = (running[2] < block_values[frame_idx : frame_idx + 1]).astype(jnp.float32)
        select = jnp.maximum(advance, flag_values[frame_idx])
        collected.append(running[0] + select * running[1] + frame_states[frame_idx])
        running = combine(
            running, frame_element(frame_states, flag_values, block_values, frame_idx)
        )
    return jnp.stack(collected)


def local(queries, keys, values, flags, blocks, out_weight, norm_gain):
    frames, lat_rows, lat_cols, model_width = queries.shape
    tokens = lat_rows * lat_cols
    key_pos = jax.nn.relu(keys).reshape(frames, tokens, HEADS, HD)
    value_heads = values.reshape(frames, tokens, HEADS, HD)
    partial_value = jnp.einsum(
        "ftha,fthb->fhab", key_pos, value_heads, preferred_element_type=jnp.float32
    )
    partial_value = partial_value.reshape(frames, HEADS * HD * HD)
    flag_values = flags.astype(jnp.float32)
    block_values = blocks.astype(jnp.float32)
    summed = lax.psum(partial_value, "row")
    totals = fold_frames(summed, flag_values, block_values)
    prefix = entering(
        (totals[0], totals[1], totals[2]), "frm", combine, empty_carry(summed.shape[1])
    )
    read_states = read_frames(prefix, summed, flag_values, block_values)
    read_tensor = read_states.reshape(frames, HEADS, HD, HD)
    query_pos = jax.nn.relu(queries).reshape(frames, tokens, HEADS, HD).astype(jnp.float32)
    attended = jnp.einsum(
        "ftha,fhab->fthb", query_pos, read_tensor, precision=lax.Precision.HIGHEST
    )
    inv_rms = lax.rsqrt(jnp.mean(attended * attended, axis=-1, keepdims=True) + norm_eps)
    gain_table = norm_gain.reshape(HEADS, HD)
    normed = (
        (attended * inv_rms * gain_table).astype(jnp.bfloat16).reshape(frames * tokens, model_width)
    )
    projected = jnp.dot(
        normed,
        lax.all_gather(out_weight, "frm", axis=0, tiled=True),
        preferred_element_type=jnp.float32,
    )
    return projected.astype(jnp.bfloat16).reshape(frames, lat_rows, lat_cols, model_width)


MESH = pl.DeviceIdType.MESH
F32 = jnp.float32
BF16 = jnp.bfloat16


def round_up(size, unit):
    return (size + unit - 1) // unit * unit


def fused(
    planes, grp_axis, frm_axis, row_axis,
    q_hbm, k_hbm, v_hbm, w_hbm, gain_ref, flag_ref, block_ref, out_ref,
    qv, kv, vv, wv, part, sent, mate_in, x_out, x_in, own, chain_in, chain_out, reads, normed,
    load_sem, zs_up, zs_dn, zr, xs, xr, ys, yr, ds, dr, ms, mr,
    ps, pr, qs, qr, cs, cr, gs, gr,
):
    g, z, r = lax.axis_index(grp_axis), lax.axis_index(frm_axis), lax.axis_index(row_axis)
    x, c = r // 2, r % 2
    mate = (g, z, 2 * x + 1 - c)
    xn = (g, z, 2 * (1 - x) + c)
    yn = (1 - g, z, r)
    up = (g, z + 1, r)
    dn = (g, z - 1, r)
    p_own, p_x, p_y, p_d = 2 * x + g, 2 * (1 - x) + g, 2 * x + 1 - g, 2 * (1 - x) + 1 - g
    frames, tokens, width = qv.shape
    groups, per = part.shape[0], part.shape[1]
    rows, cols = wv.shape[1] // 4, wv.shape[2] // 2
    depth = normed.shape[2]

    def cut(p, core):
        return (
            pl.ds(pl.multiple_of(p * rows, 16), rows),
            pl.ds(pl.multiple_of(core * cols, 128), cols),
        )

    def piece(s, p, core):
        return wv.at[(s,) + cut(p, core)]

    def remote(src, dst, send, recv, to):
        return pltpu.make_async_remote_copy(
            src_ref=src, dst_ref=dst, send_sem=send, recv_sem=recv,
            device_id=to, device_id_type=MESH,
        )

    barrier = pltpu.get_barrier_semaphore()
    for other in (mate, xn, yn):
        pl.semaphore_signal(barrier, inc=1, device_id=other, device_id_type=MESH)

    @pl.when(z > 0)
    def _():
        pl.semaphore_signal(barrier, inc=1, device_id=dn, device_id_type=MESH)

    @pl.when(z < planes - 1)
    def _():
        pl.semaphore_signal(barrier, inc=1, device_id=up, device_id_type=MESH)

    loads = [
        pltpu.make_async_copy(k_hbm, kv, load_sem.at[0]),
        pltpu.make_async_copy(v_hbm, vv, load_sem.at[1]),
        pltpu.make_async_copy(q_hbm, qv, load_sem.at[2]),
        pltpu.make_async_copy(w_hbm, wv.at[z], load_sem.at[3]),
    ]
    for load in loads:
        load.start()
    inner = (z > 0) & (z < planes - 1)

    @pl.when(inner)
    def _():
        pl.semaphore_wait(barrier, 5)

    @pl.when(jnp.logical_not(inner))
    def _():
        pl.semaphore_wait(barrier, 4)

    def first_up():
        return remote(w_hbm.at[cut(p_own, c)], piece(z, p_own, c), zs_up.at[z], zr.at[z], up)

    def first_dn():
        return remote(w_hbm.at[cut(p_own, c)], piece(z, p_own, c), zs_dn.at[z], zr.at[z], dn)

    @pl.when(z < planes - 1)
    def _():
        first_up().start()

    @pl.when(z > 0)
    def _():
        first_dn().start()

    def shard_at(i):
        near = jnp.minimum(z, planes - 1 - z)
        s = jnp.where(i - 1 >= near, i, i - 1)
        return jnp.where(z * 2 < planes, s, planes - 1 - s)

    def z_up(s):
        return remote(piece(s, p_own, c), piece(s, p_own, c), zs_up.at[s], zr.at[s], up)

    def z_dn(s):
        return remote(piece(s, p_own, c), piece(s, p_own, c), zs_dn.at[s], zr.at[s], dn)

    def x_copy(s):
        return remote(piece(s, p_own, c), piece(s, p_own, c), xs.at[s], xr.at[s], xn)

    def y_copy(s):
        return remote(piece(s, p_own, c), piece(s, p_own, c), ys.at[s], yr.at[s], yn)

    def d_copy(s):
        return remote(piece(s, p_x, c), piece(s, p_x, c), ds.at[s], dr.at[s], yn)

    def m_copy(s, kind):
        p = (p_own, p_x, p_y, p_d)[kind]
        return remote(piece(s, p, c), piece(s, p, c), ms.at[s, kind], mr.at[s, kind], mate)

    def landed(s, p, core, sem):
        pltpu.make_async_copy(piece(s, p, core), piece(s, p, core), sem).wait()

    def stage_z(i):
        s = shard_at(i)
        landed(s, p_own, c, zr.at[s])

        @pl.when((s < z) & (z < planes - 1))
        def _():
            z_up(s).start()

        @pl.when((s > z) & (z > 0))
        def _():
            z_dn(s).start()

        x_copy(s).start()
        y_copy(s).start()
        m_copy(s, 0).start()

    def stage_xy(i):
        s = shard_at(i)
        landed(s, p_x, c, xr.at[s])
        d_copy(s).start()
        m_copy(s, 1).start()
        landed(s, p_y, c, yr.at[s])
        m_copy(s, 2).start()

    def stage_d(i):
        s = shard_at(i)
        landed(s, p_d, c, dr.at[s])
        m_copy(s, 3).start()

    def stage_m(i):
        s = shard_at(i)
        for kind, p in enumerate((p_own, p_x, p_y, p_d)):
            landed(s, p, 1 - c, mr.at[s, kind])

    def finish(i):
        s = shard_at(i)

        @pl.when((s < z) & (z < planes - 1))
        def _():
            z_up(s).wait_send()

        @pl.when((s > z) & (z > 0))
        def _():
            z_dn(s).wait_send()

        x_copy(s).wait_send()
        y_copy(s).wait_send()
        d_copy(s).wait_send()
        for kind in range(4):
            m_copy(s, kind).wait_send()

    loads[0].wait()
    loads[1].wait()

    def state_step(f, carry):
        for h in range(groups * per):
            lanes = slice(h * HD, (h + 1) * HD)
            key = jnp.maximum(kv[f, :, lanes], jnp.zeros((), BF16))
            state = lax.dot_general(
                key, vv[f, :, lanes], (((0,), (0,)), ((), ())), preferred_element_type=F32
            )
            part[h // per, h % per, f] = state
            sent[h // per, h % per, f] = state.astype(BF16)
        return carry

    lax.fori_loop(0, frames, state_step, 0)

    mate_sums = [
        remote(sent.at[2 * chip + 1 - c], mate_in.at[chip], ps.at[chip], pr.at[chip], mate)
        for chip in range(groups // 2)
    ]
    for copy in mate_sums:
        copy.start()
    for copy in mate_sums:
        copy.wait_recv()
    x_out[...] = (part[2 * (1 - x) + c] + mate_in[1 - x].astype(F32)).astype(BF16)
    x_sum = remote(x_out, x_in, qs, qr, xn)
    x_sum.start()
    own[...] = part[r] + mate_in[x].astype(F32)
    stage_z(1)
    x_sum.wait_recv()

    @pl.when(z == 0)
    def _():
        chain_in[:, :, :HD, :] = jnp.zeros((per, 2, HD, HD), BF16)
        chain_in[:, :, HD:, :] = jnp.full((per, 2, chain_in.shape[2] - HD, HD), -1.0, BF16)

    def chain_copy(h):
        return remote(chain_out.at[h], chain_in.at[h], cs.at[h], cr.at[h], up)

    for h in range(per):

        @pl.when(z > 0)
        def _():
            pltpu.make_async_copy(chain_in.at[h], chain_in.at[h], cr.at[h]).wait()

        closed = chain_in[h, 0, :HD, :].astype(F32)
        opened = chain_in[h, 1, :HD, :].astype(F32)
        latest = chain_in[h, 0, HD:, :].astype(F32)[:1]
        for f in range(frames):
            summed = own[h, f] + x_in[h, f].astype(F32)
            flag = flag_ref[f].astype(F32)
            block = block_ref[f].astype(F32)
            advance = jnp.where(latest < block, 1.0, 0.0)
            select = jnp.maximum(advance, flag)
            reads[r, h, f] = (closed + select * opened + summed).astype(BF16)
            closed = closed + advance * opened
            opened = flag * summed + (1.0 - advance) * opened
            latest = jnp.maximum(latest, block)

        @pl.when(z < planes - 1)
        def _():
            chain_out[h, 0, :HD, :] = closed.astype(BF16)
            chain_out[h, 1, :HD, :] = opened.astype(BF16)
            chain_out[h, 0, HD:, :] = jnp.broadcast_to(
                latest, (chain_in.shape[2] - HD, HD)
            ).astype(BF16)
            chain_copy(h).start()

    other_x = 2 * (1 - x) + c
    read_mate = remote(reads.at[r], reads.at[r], gs.at[0], gr.at[0], mate)
    read_x = remote(reads.at[r], reads.at[r], gs.at[1], gr.at[1], xn)
    relay = remote(reads.at[other_x], reads.at[other_x], gs.at[2], gr.at[2], mate)
    read_x.start()
    read_mate.start()
    stage_xy(1)
    stage_z(2)

    def got(group, sem):
        pltpu.make_async_copy(reads.at[group], reads.at[group], sem).wait()

    got(other_x, gr.at[1])
    relay.start()
    stage_d(1)
    stage_xy(2)
    stage_z(3) if planes > 3 else None
    got(2 * x + 1 - c, gr.at[0])
    got(2 * (1 - x) + 1 - c, gr.at[2])
    loads[2].wait()

    def read_step(f, carry):
        for h in range(groups * per):
            lanes = slice(h * HD, (h + 1) * HD)
            query = jnp.maximum(qv[f, :, lanes], jnp.zeros((), BF16))
            attended = jnp.dot(
                query, reads[h // per, h % per, f], preferred_element_type=F32
            )
            mean = jnp.sum(attended * attended, axis=-1, keepdims=True) * (1.0 / HD)
            value = attended * lax.rsqrt(mean + norm_eps) * gain_ref[h : h + 1, :]
            at = h * HD % depth
            normed[h * HD // depth, pl.ds(pl.multiple_of(f * tokens, tokens), tokens), at : at + HD] = (
                value.astype(BF16)
            )
        return carry

    lax.fori_loop(0, frames, read_step, 0)
    for i in range(4, planes):
        stage_z(i)
    for i in range(3, planes):
        stage_xy(i)
    for i in range(2, planes):
        stage_d(i)
    for i in range(1, planes):
        stage_m(i)
    loads[3].wait()

    def project(lanes):
        total = jnp.dot(normed[0], wv[0, :depth, lanes], preferred_element_type=F32)
        for s in range(1, planes):
            total += jnp.dot(normed[s], wv[s, :depth, lanes], preferred_element_type=F32)
        out_ref[:, lanes] = total.astype(BF16)

    tile = 256

    def project_step(n, carry):
        project(pl.ds(pl.multiple_of(n * tile, tile), tile))
        return carry

    lax.fori_loop(0, width // tile, project_step, 0)
    if width % tile:
        project(slice(width // tile * tile, width))

    @pl.when(z < planes - 1)
    def _():
        first_up().wait_send()
        for h in range(per):
            chain_copy(h).wait_send()

    @pl.when(z > 0)
    def _():
        first_dn().wait_send()

    for i in range(1, planes):
        finish(i)
    for copy in mate_sums:
        copy.wait_send()
    x_sum.wait_send()
    read_mate.wait_send()
    read_x.wait_send()
    relay.wait_send()


def local_fused(mesh_shape, queries, keys, values, flags, blocks, out_weight, norm_gain):
    frames, lat_rows, lat_cols, width = queries.shape
    tokens = lat_rows * lat_cols
    planes, groups = mesh_shape["frm"], mesh_shape["row"]
    per = HEADS // groups
    depth = out_weight.shape[0]
    rows, cols = round_up(depth, 64), round_up(width, 256)
    weight = jnp.pad(out_weight, ((0, rows - depth), (0, cols - width)))
    dma = pltpu.SemaphoreType.DMA
    shape = (frames, tokens, width)
    anywhere = pl.BlockSpec(memory_space=pl.ANY)
    scalar = pl.BlockSpec(memory_space=pltpu.SMEM)
    vector = pl.BlockSpec(memory_space=pltpu.VMEM)
    per_group = (per, frames, HD, HD)
    link = (per, 2, round_up(HD + 1, 16), HD)
    out = pl.pallas_call(
        functools.partial(fused, planes, "grp", "frm", "row"),
        out_shape=jax.ShapeDtypeStruct((frames * tokens, width), BF16),
        in_specs=[anywhere] * 4 + [vector, scalar, scalar],
        out_specs=vector,
        scratch_shapes=[
            pltpu.VMEM(shape, BF16),
            pltpu.VMEM(shape, BF16),
            pltpu.VMEM(shape, BF16),
            pltpu.VMEM((planes, rows, cols), BF16),
            pltpu.VMEM((groups,) + per_group, F32),
            pltpu.VMEM((groups,) + per_group, BF16),
            pltpu.VMEM((groups // 2,) + per_group, BF16),
            pltpu.VMEM(per_group, BF16),
            pltpu.VMEM(per_group, BF16),
            pltpu.VMEM(per_group, F32),
            pltpu.VMEM(link, BF16),
            pltpu.VMEM(link, BF16),
            pltpu.VMEM((groups,) + per_group, BF16),
            pltpu.VMEM((planes, frames * tokens, depth), BF16),
            dma((4,)),
        ]
        + [dma((planes,))] * 9
        + [dma((planes, 4))] * 2
        + [dma((groups // 2,))] * 2
        + [dma(()), dma(())]
        + [dma((per,))] * 2
        + [dma((3,))] * 2,
        compiler_params=pltpu.CompilerParams(
            collective_id=0, has_side_effects=True, vmem_limit_bytes=56 * 1024 * 1024
        ),
    )(
        queries.reshape(shape), keys.reshape(shape), values.reshape(shape), weight,
        norm_gain.reshape(HEADS, HD), flags, blocks,
    )
    return out.reshape(queries.shape)


def fits(mesh):
    grp, frm, row = mesh.shape["grp"], mesh.shape["frm"], mesh.shape["row"]
    return grp == 2 and row == 4 and frm > 2 and HEADS % row == 0 and HEADS % frm == 0


def solution(mesh):
    in_specs = (
        P(("grp", "frm"), "row", None, None),
        P(("grp", "frm"), "row", None, None),
        P(("grp", "frm"), "row", None, None),
        P(("grp", "frm")),
        P(("grp", "frm")),
        P("frm", None),
        P(),
    )
    out_specs = P(("grp", "frm"), "row", None, None)
    body = functools.partial(local_fused, dict(mesh.shape)) if fits(mesh) else local
    return jax.shard_map(body, mesh=mesh, in_specs=in_specs, out_specs=out_specs, check_vma=False)
```

```python
import functools

import jax
import jax.numpy as jnp
from jax import lax
from jax.sharding import PartitionSpec as P
from jax.experimental import pallas as pl
from jax.experimental.pallas import tpu as pltpu

HEADS = 20
HD = 112


norm_eps = 1e-06


def entering(part, axis, combine, identity):
    place = lax.axis_index(axis)
    gathered = jax.tree.map(lambda a: lax.all_gather(a, axis), part)
    state = jax.tree.map(lambda a, e: jnp.zeros_like(a) + jnp.asarray(e, a.dtype), part, identity)

    def one(step, state):
        return combine(
            state, jax.tree.map(lambda a: lax.dynamic_index_in_dim(a, step, 0, False), gathered)
        )

    return lax.fori_loop(0, place, one, state)


def combine(earlier, later):
    closed_a, opened_a, latest_a = earlier
    closed_b, opened_b, latest_b = later
    advance = (latest_a < latest_b).astype(jnp.float32)
    return (
        closed_a + closed_b + advance * opened_a,
        opened_b + (1.0 - advance) * opened_a,
        jnp.maximum(latest_a, latest_b),
    )


def empty_carry(length):
    return (
        jnp.zeros((length,), jnp.float32),
        jnp.zeros((length,), jnp.float32),
        jnp.full((1,), -1.0, jnp.float32),
    )


def frame_element(frame_states, flag_values, block_values, frame_idx):
    length = frame_states.shape[1]
    return (
        jnp.zeros((length,), jnp.float32),
        flag_values[frame_idx] * frame_states[frame_idx],
        block_values[frame_idx : frame_idx + 1],
    )


def fold_frames(frame_states, flag_values, block_values):
    running = empty_carry(frame_states.shape[1])
    for frame_idx in range(frame_states.shape[0]):
        running = combine(
            running, frame_element(frame_states, flag_values, block_values, frame_idx)
        )
    return running


def read_frames(prefix, frame_states, flag_values, block_values):
    running = prefix
    collected = []
    for frame_idx in range(frame_states.shape[0]):
        advance = (running[2] < block_values[frame_idx : frame_idx + 1]).astype(jnp.float32)
        select = jnp.maximum(advance, flag_values[frame_idx])
        collected.append(running[0] + select * running[1] + frame_states[frame_idx])
        running = combine(
            running, frame_element(frame_states, flag_values, block_values, frame_idx)
        )
    return jnp.stack(collected)


def local(queries, keys, values, flags, blocks, out_weight, norm_gain):
    frames, lat_rows, lat_cols, model_width = queries.shape
    tokens = lat_rows * lat_cols
    key_pos = jax.nn.relu(keys).reshape(frames, tokens, HEADS, HD)
    value_heads = values.reshape(frames, tokens, HEADS, HD)
    partial_value = jnp.einsum(
        "ftha,fthb->fhab", key_pos, value_heads, preferred_element_type=jnp.float32
    )
    partial_value = partial_value.reshape(frames, HEADS * HD * HD)
    flag_values = flags.astype(jnp.float32)
    block_values = blocks.astype(jnp.float32)
    summed = lax.psum(partial_value, "row")
    totals = fold_frames(summed, flag_values, block_values)
    prefix = entering(
        (totals[0], totals[1], totals[2]), "frm", combine, empty_carry(summed.shape[1])
    )
    read_states = read_frames(prefix, summed, flag_values, block_values)
    read_tensor = read_states.reshape(frames, HEADS, HD, HD)
    query_pos = jax.nn.relu(queries).reshape(frames, tokens, HEADS, HD).astype(jnp.float32)
    attended = jnp.einsum(
        "ftha,fhab->fthb", query_pos, read_tensor, precision=lax.Precision.HIGHEST
    )
    inv_rms = lax.rsqrt(jnp.mean(attended * attended, axis=-1, keepdims=True) + norm_eps)
    gain_table = norm_gain.reshape(HEADS, HD)
    normed = (
        (attended * inv_rms * gain_table).astype(jnp.bfloat16).reshape(frames * tokens, model_width)
    )
    projected = jnp.dot(
        normed,
        lax.all_gather(out_weight, "frm", axis=0, tiled=True),
        preferred_element_type=jnp.float32,
    )
    return projected.astype(jnp.bfloat16).reshape(frames, lat_rows, lat_cols, model_width)


MESH = pl.DeviceIdType.MESH
F32 = jnp.float32
BF16 = jnp.bfloat16


def round_up(size, unit):
    return (size + unit - 1) // unit * unit


def fused(
    planes, grp_axis, frm_axis, row_axis,
    q_hbm, k_hbm, v_hbm, w_hbm, gain_ref, flag_ref, block_ref, out_ref,
    qv, kv, vv, wv, part, sent, mate_in, x_out, x_in, own, chain_in, chain_out, reads, normed, gains,
    load_sem, zs_up, zs_dn, zr, xs, xr, ys, yr, ds, dr, ms, mr,
    ps, pr, qs, qr, cs, cr, gs, gr,
):
    g, z, r = lax.axis_index(grp_axis), lax.axis_index(frm_axis), lax.axis_index(row_axis)
    x, c = r // 2, r % 2
    mate = (g, z, 2 * x + 1 - c)
    xn = (g, z, 2 * (1 - x) + c)
    yn = (1 - g, z, r)
    up = (g, z + 1, r)
    dn = (g, z - 1, r)
    p_own, p_x, p_y, p_d = 2 * x + g, 2 * (1 - x) + g, 2 * x + 1 - g, 2 * (1 - x) + 1 - g
    frames, lat_rows, width, lat_cols = qv.shape
    tokens = lat_rows * lat_cols
    groups, per = part.shape[0], part.shape[1]
    rows, cols = wv.shape[1] // 4, wv.shape[2] // 2
    depth = normed.shape[1]

    def cut(p, core):
        return (
            pl.ds(pl.multiple_of(p * rows, 16), rows),
            pl.ds(pl.multiple_of(core * cols, 128), cols),
        )

    def piece(s, p, core):
        return wv.at[(s,) + cut(p, core)]

    def remote(src, dst, send, recv, to):
        return pltpu.make_async_remote_copy(
            src_ref=src, dst_ref=dst, send_sem=send, recv_sem=recv,
            device_id=to, device_id_type=MESH,
        )

    barrier = pltpu.get_barrier_semaphore()
    for other in (mate, xn, yn):
        pl.semaphore_signal(barrier, inc=1, device_id=other, device_id_type=MESH)

    @pl.when(z > 0)
    def _():
        pl.semaphore_signal(barrier, inc=1, device_id=dn, device_id_type=MESH)

    @pl.when(z < planes - 1)
    def _():
        pl.semaphore_signal(barrier, inc=1, device_id=up, device_id_type=MESH)

    loads = [
        pltpu.make_async_copy(k_hbm, kv, load_sem.at[0]),
        pltpu.make_async_copy(v_hbm, vv, load_sem.at[1]),
        pltpu.make_async_copy(q_hbm, qv, load_sem.at[2]),
        pltpu.make_async_copy(w_hbm, wv.at[z], load_sem.at[3]),
    ]
    for load in loads:
        load.start()
    inner = (z > 0) & (z < planes - 1)

    @pl.when(inner)
    def _():
        pl.semaphore_wait(barrier, 5)

    @pl.when(jnp.logical_not(inner))
    def _():
        pl.semaphore_wait(barrier, 4)

    def first_up():
        return remote(w_hbm.at[cut(p_own, c)], piece(z, p_own, c), zs_up.at[z], zr.at[z], up)

    def first_dn():
        return remote(w_hbm.at[cut(p_own, c)], piece(z, p_own, c), zs_dn.at[z], zr.at[z], dn)

    @pl.when(z < planes - 1)
    def _():
        first_up().start()

    @pl.when(z > 0)
    def _():
        first_dn().start()

    def shard_at(i):
        near = jnp.minimum(z, planes - 1 - z)
        s = jnp.where(i - 1 >= near, i, i - 1)
        return jnp.where(z * 2 < planes, s, planes - 1 - s)

    def z_up(s):
        return remote(piece(s, p_own, c), piece(s, p_own, c), zs_up.at[s], zr.at[s], up)

    def z_dn(s):
        return remote(piece(s, p_own, c), piece(s, p_own, c), zs_dn.at[s], zr.at[s], dn)

    def x_copy(s):
        return remote(piece(s, p_own, c), piece(s, p_own, c), xs.at[s], xr.at[s], xn)

    def y_copy(s):
        return remote(piece(s, p_own, c), piece(s, p_own, c), ys.at[s], yr.at[s], yn)

    def d_copy(s):
        return remote(piece(s, p_x, c), piece(s, p_x, c), ds.at[s], dr.at[s], yn)

    def m_copy(s, kind):
        p = (p_own, p_x, p_y, p_d)[kind]
        return remote(piece(s, p, c), piece(s, p, c), ms.at[s, kind], mr.at[s, kind], mate)

    def landed(s, p, core, sem):
        pltpu.make_async_copy(piece(s, p, core), piece(s, p, core), sem).wait()

    def stage_z(i):
        s = shard_at(i)
        landed(s, p_own, c, zr.at[s])

        @pl.when((s < z) & (z < planes - 1))
        def _():
            z_up(s).start()

        @pl.when((s > z) & (z > 0))
        def _():
            z_dn(s).start()

        x_copy(s).start()
        y_copy(s).start()
        m_copy(s, 0).start()

    def stage_xy(i):
        s = shard_at(i)
        landed(s, p_x, c, xr.at[s])
        d_copy(s).start()
        m_copy(s, 1).start()
        landed(s, p_y, c, yr.at[s])
        m_copy(s, 2).start()

    def stage_d(i):
        s = shard_at(i)
        landed(s, p_d, c, dr.at[s])
        m_copy(s, 3).start()

    def stage_m(i):
        s = shard_at(i)
        for kind, p in enumerate((p_own, p_x, p_y, p_d)):
            landed(s, p, 1 - c, mr.at[s, kind])

    def finish(i):
        s = shard_at(i)

        @pl.when((s < z) & (z < planes - 1))
        def _():
            z_up(s).wait_send()

        @pl.when((s > z) & (z > 0))
        def _():
            z_dn(s).wait_send()

        x_copy(s).wait_send()
        y_copy(s).wait_send()
        d_copy(s).wait_send()
        for kind in range(4):
            m_copy(s, kind).wait_send()

    loads[0].wait()
    loads[1].wait()

    def head_of(ref, f, h):
        span = slice(h * HD, (h + 1) * HD)
        return jnp.concatenate([ref[f, row, span, :] for row in range(lat_rows)], axis=1)

    def state_step(f, carry):
        for h in range(groups * per):
            key = jnp.maximum(head_of(kv, f, h), jnp.zeros((), BF16))
            state = lax.dot_general(
                head_of(vv, f, h), key, (((1,), (1,)), ((), ())), preferred_element_type=F32
            )
            part[h // per, h % per, f] = state
            sent[h // per, h % per, f] = state.astype(BF16)
        return carry

    lax.fori_loop(0, frames, state_step, 0)

    mate_sums = [
        remote(sent.at[2 * chip + 1 - c], mate_in.at[chip], ps.at[chip], pr.at[chip], mate)
        for chip in range(groups // 2)
    ]
    for copy in mate_sums:
        copy.start()
    diagonal = (
        lax.broadcasted_iota(jnp.int32, (HD, HD), 0) == lax.broadcasted_iota(jnp.int32, (HD, HD), 1)
    ).astype(F32)
    for h in range(groups * per):
        span = slice(h * HD, (h + 1) * HD)
        gains[span, :] = jnp.sum(diagonal * gain_ref[:, span], axis=1, keepdims=True)
    for copy in mate_sums:
        copy.wait_recv()
    x_out[...] = (part[2 * (1 - x) + c] + mate_in[1 - x].astype(F32)).astype(BF16)
    x_sum = remote(x_out, x_in, qs, qr, xn)
    x_sum.start()
    own[...] = part[r] + mate_in[x].astype(F32)
    stage_z(1)
    x_sum.wait_recv()

    @pl.when(z == 0)
    def _():
        chain_in[:, :, :HD, :] = jnp.zeros((per, 2, HD, HD), BF16)
        chain_in[:, :, HD:, :] = jnp.full((per, 2, chain_in.shape[2] - HD, HD), -1.0, BF16)

    def chain_copy(h):
        return remote(chain_out.at[h], chain_in.at[h], cs.at[h], cr.at[h], up)

    upper = z * 2 >= planes

    def early():
        stage_xy(1)
        stage_z(2)

    pl.when(upper)(early)

    for h in range(per):

        @pl.when(z > 0)
        def _():
            pltpu.make_async_copy(chain_in.at[h], chain_in.at[h], cr.at[h]).wait()

        closed = chain_in[h, 0, :HD, :].astype(F32)
        opened = chain_in[h, 1, :HD, :].astype(F32)
        latest = chain_in[h, 0, HD:, :].astype(F32)[:1]
        for f in range(frames):
            summed = own[h, f] + x_in[h, f].astype(F32)
            flag = flag_ref[f].astype(F32)
            block = block_ref[f].astype(F32)
            advance = jnp.where(latest < block, 1.0, 0.0)
            select = jnp.maximum(advance, flag)
            reads[r, h, f] = (closed + select * opened + summed).astype(BF16)
            closed = closed + advance * opened
            opened = flag * summed + (1.0 - advance) * opened
            latest = jnp.maximum(latest, block)

        @pl.when(z < planes - 1)
        def _():
            chain_out[h, 0, :HD, :] = closed.astype(BF16)
            chain_out[h, 1, :HD, :] = opened.astype(BF16)
            chain_out[h, 0, HD:, :] = jnp.broadcast_to(
                latest, (chain_in.shape[2] - HD, HD)
            ).astype(BF16)
            chain_copy(h).start()

    other_x = 2 * (1 - x) + c
    read_mate = remote(reads.at[r], reads.at[r], gs.at[0], gr.at[0], mate)
    read_x = remote(reads.at[r], reads.at[r], gs.at[1], gr.at[1], xn)
    relay = remote(reads.at[other_x], reads.at[other_x], gs.at[2], gr.at[2], mate)
    read_x.start()
    read_mate.start()
    pl.when(jnp.logical_not(upper))(early)

    def got(group, sem):
        pltpu.make_async_copy(reads.at[group], reads.at[group], sem).wait()

    got(other_x, gr.at[1])
    relay.start()
    stage_d(1)
    stage_xy(2)
    stage_z(3) if planes > 3 else None
    got(2 * x + 1 - c, gr.at[0])
    got(2 * (1 - x) + 1 - c, gr.at[2])
    loads[2].wait()

    def read_step(f, carry):
        for h in range(groups * per):
            query = jnp.maximum(head_of(qv, f, h), jnp.zeros((), BF16))
            attended = jnp.dot(
                reads[h // per, h % per, f], query, preferred_element_type=F32
            )
            mean = jnp.sum(attended * attended, axis=0, keepdims=True) * (1.0 / HD)
            value = attended * lax.rsqrt(mean + norm_eps) * gains[h * HD : (h + 1) * HD, :]
            at = h * HD % depth
            normed[h * HD // depth, at : at + HD, pl.ds(pl.multiple_of(f * tokens, tokens), tokens)] = (
                value.astype(BF16)
            )
        return carry

    lax.fori_loop(0, frames, read_step, 0)
    for i in range(4, planes):
        stage_z(i)
    for i in range(3, planes):
        stage_xy(i)
    for i in range(2, planes):
        stage_d(i)
    for i in range(1, planes):
        stage_m(i)
    loads[3].wait()

    def product(s, lanes):
        return lax.dot_general(
            wv[s, :depth, lanes], normed[s], (((0,), (0,)), ((), ())), preferred_element_type=F32
        )

    def project(lanes):
        total = product(0, lanes)
        for s in range(1, planes):
            total += product(s, lanes)
        for f in range(frames):
            for row in range(lat_rows):
                at = (f * lat_rows + row) * lat_cols
                out_ref[f, row, lanes, :] = total[:, at : at + lat_cols].astype(BF16)

    tile = 256

    def project_step(n, carry):
        project(pl.ds(pl.multiple_of(n * tile, tile), tile))
        return carry

    lax.fori_loop(0, width // tile, project_step, 0)
    if width % tile:
        project(slice(width // tile * tile, width))

    @pl.when(z < planes - 1)
    def _():
        first_up().wait_send()
        for h in range(per):
            chain_copy(h).wait_send()

    @pl.when(z > 0)
    def _():
        first_dn().wait_send()

    for i in range(1, planes):
        finish(i)
    for copy in mate_sums:
        copy.wait_send()
    x_sum.wait_send()
    read_mate.wait_send()
    read_x.wait_send()
    relay.wait_send()


def local_fused(mesh_shape, queries, keys, values, flags, blocks, out_weight, norm_gain):
    frames, lat_rows, lat_cols, width = queries.shape
    planes, groups = mesh_shape["frm"], mesh_shape["row"]
    per = HEADS // groups
    depth = out_weight.shape[0]
    rows, cols = round_up(depth, 64), round_up(width, 256)
    weight = jnp.pad(out_weight, ((0, rows - depth), (0, cols - width)))
    dma = pltpu.SemaphoreType.DMA
    shape = (frames, lat_rows, width, lat_cols)
    anywhere = pl.BlockSpec(memory_space=pl.ANY)
    scalar = pl.BlockSpec(memory_space=pltpu.SMEM)
    vector = pl.BlockSpec(memory_space=pltpu.VMEM)
    per_group = (per, frames, HD, HD)
    link = (per, 2, round_up(HD + 1, 16), HD)
    out = pl.pallas_call(
        functools.partial(fused, planes, "grp", "frm", "row"),
        out_shape=jax.ShapeDtypeStruct(shape, BF16),
        in_specs=[anywhere] * 4 + [vector, scalar, scalar],
        out_specs=vector,
        scratch_shapes=[
            pltpu.VMEM(shape, BF16),
            pltpu.VMEM(shape, BF16),
            pltpu.VMEM(shape, BF16),
            pltpu.VMEM((planes, rows, cols), BF16),
            pltpu.VMEM((groups,) + per_group, F32),
            pltpu.VMEM((groups,) + per_group, BF16),
            pltpu.VMEM((groups // 2,) + per_group, BF16),
            pltpu.VMEM(per_group, BF16),
            pltpu.VMEM(per_group, BF16),
            pltpu.VMEM(per_group, F32),
            pltpu.VMEM(link, BF16),
            pltpu.VMEM(link, BF16),
            pltpu.VMEM((groups,) + per_group, BF16),
            pltpu.VMEM((planes, depth, frames * lat_rows * lat_cols), BF16),
            pltpu.VMEM((width, 1), F32),
            dma((4,)),
        ]
        + [dma((planes,))] * 9
        + [dma((planes, 4))] * 2
        + [dma((groups // 2,))] * 2
        + [dma(()), dma(())]
        + [dma((per,))] * 2
        + [dma((3,))] * 2,
        compiler_params=pltpu.CompilerParams(
            collective_id=0, has_side_effects=True, vmem_limit_bytes=56 * 1024 * 1024
        ),
    )(
        *(jnp.swapaxes(a, 2, 3) for a in (queries, keys, values)), weight,
        norm_gain.reshape(1, width), flags, blocks,
    )
    return jnp.swapaxes(out, 2, 3)


def fits(mesh):
    grp, frm, row = mesh.shape["grp"], mesh.shape["frm"], mesh.shape["row"]
    return grp == 2 and row == 4 and frm > 2 and HEADS % row == 0 and HEADS % frm == 0


def solution(mesh):
    in_specs = (
        P(("grp", "frm"), "row", None, None),
        P(("grp", "frm"), "row", None, None),
        P(("grp", "frm"), "row", None, None),
        P(("grp", "frm")),
        P(("grp", "frm")),
        P("frm", None),
        P(),
    )
    out_specs = P(("grp", "frm"), "row", None, None)
    body = functools.partial(local_fused, dict(mesh.shape)) if fits(mesh) else local
    return jax.shard_map(body, mesh=mesh, in_specs=in_specs, out_specs=out_specs, check_vma=False)
```

```python
import functools

import jax
import jax.numpy as jnp
from jax import lax
from jax.sharding import PartitionSpec as P
from jax.experimental import pallas as pl
from jax.experimental.pallas import tpu as pltpu

HEADS = 20
HD = 112


norm_eps = 1e-06
CHUNKS = 3


def entering(part, axis, combine, identity):
    place = lax.axis_index(axis)
    gathered = jax.tree.map(lambda a: lax.all_gather(a, axis), part)
    state = jax.tree.map(lambda a, e: jnp.zeros_like(a) + jnp.asarray(e, a.dtype), part, identity)

    def one(step, state):
        return combine(
            state, jax.tree.map(lambda a: lax.dynamic_index_in_dim(a, step, 0, False), gathered)
        )

    return lax.fori_loop(0, place, one, state)


def combine(earlier, later):
    closed_a, opened_a, latest_a = earlier
    closed_b, opened_b, latest_b = later
    advance = (latest_a < latest_b).astype(jnp.float32)
    return (
        closed_a + closed_b + advance * opened_a,
        opened_b + (1.0 - advance) * opened_a,
        jnp.maximum(latest_a, latest_b),
    )


def empty_carry(length):
    return (
        jnp.zeros((length,), jnp.float32),
        jnp.zeros((length,), jnp.float32),
        jnp.full((1,), -1.0, jnp.float32),
    )


def frame_element(frame_states, flag_values, block_values, frame_idx):
    length = frame_states.shape[1]
    return (
        jnp.zeros((length,), jnp.float32),
        flag_values[frame_idx] * frame_states[frame_idx],
        block_values[frame_idx : frame_idx + 1],
    )


def fold_frames(frame_states, flag_values, block_values):
    running = empty_carry(frame_states.shape[1])
    for frame_idx in range(frame_states.shape[0]):
        running = combine(
            running, frame_element(frame_states, flag_values, block_values, frame_idx)
        )
    return running


def read_frames(prefix, frame_states, flag_values, block_values):
    running = prefix
    collected = []
    for frame_idx in range(frame_states.shape[0]):
        advance = (running[2] < block_values[frame_idx : frame_idx + 1]).astype(jnp.float32)
        select = jnp.maximum(advance, flag_values[frame_idx])
        collected.append(running[0] + select * running[1] + frame_states[frame_idx])
        running = combine(
            running, frame_element(frame_states, flag_values, block_values, frame_idx)
        )
    return jnp.stack(collected)


def local(queries, keys, values, flags, blocks, out_weight, norm_gain):
    frames, lat_rows, lat_cols, model_width = queries.shape
    tokens = lat_rows * lat_cols
    key_pos = jax.nn.relu(keys).reshape(frames, tokens, HEADS, HD)
    value_heads = values.reshape(frames, tokens, HEADS, HD)
    partial_value = jnp.einsum(
        "ftha,fthb->fhab", key_pos, value_heads, preferred_element_type=jnp.float32
    )
    partial_value = partial_value.reshape(frames, HEADS * HD * HD)
    flag_values = flags.astype(jnp.float32)
    block_values = blocks.astype(jnp.float32)
    summed = lax.psum(partial_value, "row")
    totals = fold_frames(summed, flag_values, block_values)
    prefix = entering(
        (totals[0], totals[1], totals[2]), "frm", combine, empty_carry(summed.shape[1])
    )
    read_states = read_frames(prefix, summed, flag_values, block_values)
    read_tensor = read_states.reshape(frames, HEADS, HD, HD)
    query_pos = jax.nn.relu(queries).reshape(frames, tokens, HEADS, HD).astype(jnp.float32)
    attended = jnp.einsum(
        "ftha,fhab->fthb", query_pos, read_tensor, precision=lax.Precision.HIGHEST
    )
    inv_rms = lax.rsqrt(jnp.mean(attended * attended, axis=-1, keepdims=True) + norm_eps)
    gain_table = norm_gain.reshape(HEADS, HD)
    normed = (
        (attended * inv_rms * gain_table).astype(jnp.bfloat16).reshape(frames * tokens, model_width)
    )
    projected = jnp.dot(
        normed,
        lax.all_gather(out_weight, "frm", axis=0, tiled=True),
        preferred_element_type=jnp.float32,
    )
    return projected.astype(jnp.bfloat16).reshape(frames, lat_rows, lat_cols, model_width)


MESH = pl.DeviceIdType.MESH
F32 = jnp.float32
BF16 = jnp.bfloat16


def round_up(size, unit):
    return (size + unit - 1) // unit * unit


def fused(
    planes, grp_axis, frm_axis, row_axis,
    q_hbm, k_hbm, v_hbm, w_hbm, gain_ref, flag_ref, block_ref, out_ref,
    qv, kv, vv, wv, part, sent, mate_in, x_out, x_in, own, chain_in, chain_out, reads, normed, gains, acc,
    load_sem, zs_up, zs_dn, zr, xs, xr, ys, yr, ds, dr, ms, mr,
    ps, pr, qs, qr, cs, cr, gs, gr,
):
    g, z, r = lax.axis_index(grp_axis), lax.axis_index(frm_axis), lax.axis_index(row_axis)
    x, c = r // 2, r % 2
    mate = (g, z, 2 * x + 1 - c)
    xn = (g, z, 2 * (1 - x) + c)
    yn = (1 - g, z, r)
    up = (g, z + 1, r)
    dn = (g, z - 1, r)
    p_own, p_x, p_y, p_d = 2 * x + g, 2 * (1 - x) + g, 2 * x + 1 - g, 2 * (1 - x) + 1 - g
    frames, lat_rows, width, lat_cols = qv.shape
    tokens = lat_rows * lat_cols
    groups, per = part.shape[0], part.shape[1]
    rows, cols = wv.shape[1] // 4, wv.shape[2] // 2
    depth = normed.shape[1]

    chunk = rows // CHUNKS

    def cut(p, core, j):
        return (
            pl.ds(pl.multiple_of(p * rows + j * chunk, 16), chunk),
            pl.ds(pl.multiple_of(core * cols, 128), cols),
        )

    def piece(s, p, core, j):
        return wv.at[(s,) + cut(p, core, j)]

    def remote(src, dst, send, recv, to):
        return pltpu.make_async_remote_copy(
            src_ref=src, dst_ref=dst, send_sem=send, recv_sem=recv,
            device_id=to, device_id_type=MESH,
        )

    barrier = pltpu.get_barrier_semaphore()
    for other in (mate, xn, yn):
        pl.semaphore_signal(barrier, inc=1, device_id=other, device_id_type=MESH)

    @pl.when(z > 0)
    def _():
        pl.semaphore_signal(barrier, inc=1, device_id=dn, device_id_type=MESH)

    @pl.when(z < planes - 1)
    def _():
        pl.semaphore_signal(barrier, inc=1, device_id=up, device_id_type=MESH)

    loads = [
        pltpu.make_async_copy(k_hbm, kv, load_sem.at[0]),
        pltpu.make_async_copy(v_hbm, vv, load_sem.at[1]),
        pltpu.make_async_copy(q_hbm, qv, load_sem.at[2]),
        pltpu.make_async_copy(w_hbm, wv.at[z], load_sem.at[3]),
    ]
    for load in loads:
        load.start()
    inner = (z > 0) & (z < planes - 1)

    @pl.when(inner)
    def _():
        pl.semaphore_wait(barrier, 5)

    @pl.when(jnp.logical_not(inner))
    def _():
        pl.semaphore_wait(barrier, 4)

    along = [(p_own, j) for j in range(CHUNKS)] + [(p_d, 0)]

    def first_up(n):
        p, j = along[n]
        return remote(w_hbm.at[cut(p, c, j)], piece(z, p, c, j), zs_up.at[z, n], zr.at[z, n], up)

    def first_dn(n):
        p, j = along[n]
        return remote(w_hbm.at[cut(p, c, j)], piece(z, p, c, j), zs_dn.at[z, n], zr.at[z, n], dn)

    for n in range(CHUNKS + 1):

        @pl.when(z < planes - 1)
        def _():
            first_up(n).start()

        @pl.when(z > 0)
        def _():
            first_dn(n).start()

    def shard_at(i):
        near = jnp.minimum(z, planes - 1 - z)
        s = jnp.where(i - 1 >= near, i, i - 1)
        return jnp.where(z * 2 < planes, s, planes - 1 - s)

    def z_up(s, n):
        p, j = along[n]
        return remote(piece(s, p, c, j), piece(s, p, c, j), zs_up.at[s, n], zr.at[s, n], up)

    def z_dn(s, n):
        p, j = along[n]
        return remote(piece(s, p, c, j), piece(s, p, c, j), zs_dn.at[s, n], zr.at[s, n], dn)

    def x_copy(s, j):
        return remote(piece(s, p_own, c, j), piece(s, p_own, c, j), xs.at[s, j], xr.at[s, j], xn)

    def y_copy(s, j):
        return remote(piece(s, p_own, c, j), piece(s, p_own, c, j), ys.at[s, j], yr.at[s, j], yn)

    def d_copy(s, j):
        return remote(piece(s, p_x, c, j), piece(s, p_x, c, j), ds.at[s, j], dr.at[s, j], yn)

    def m_copy(s, kind, j):
        p = (p_own, p_x, p_y, p_d)[kind]
        at = kind * CHUNKS + j
        return remote(piece(s, p, c, j), piece(s, p, c, j), ms.at[s, at], mr.at[s, at], mate)

    def landed(s, p, core, j, sem):
        pltpu.make_async_copy(piece(s, p, core, j), piece(s, p, core, j), sem).wait()

    def stage_z(i, n):
        s = shard_at(i)
        p, j = along[n]
        landed(s, p, c, j, zr.at[s, n])

        @pl.when((s < z) & (z < planes - 1))
        def _():
            z_up(s, n).start()

        @pl.when((s > z) & (z > 0))
        def _():
            z_dn(s, n).start()

        if n < CHUNKS:
            y_copy(s, j).start()
            x_copy(s, j).start()
            m_copy(s, 0, j).start()
        else:
            m_copy(s, 3, j).start()

    def stage_xy(i, j):
        s = shard_at(i)
        landed(s, p_x, c, j, xr.at[s, j])
        if j > 0:
            d_copy(s, j).start()
        m_copy(s, 1, j).start()
        landed(s, p_y, c, j, yr.at[s, j])
        m_copy(s, 2, j).start()

    def stage_d(i, j):
        if j > 0:
            s = shard_at(i)
            landed(s, p_d, c, j, dr.at[s, j])
            m_copy(s, 3, j).start()

    def stage_m(i):
        s = shard_at(i)
        for kind, p in enumerate((p_own, p_x, p_y, p_d)):
            for j in range(CHUNKS):
                landed(s, p, 1 - c, j, mr.at[s, kind * CHUNKS + j])

    units = (planes - 1) * CHUNKS

    def step(k):
        if k < units:
            i, j = k // CHUNKS + 1, k % CHUNKS
            stage_z(i, j)
            if j == CHUNKS - 1:
                stage_z(i, CHUNKS)
        if 0 <= k - 2 < units:
            stage_xy((k - 2) // CHUNKS + 1, (k - 2) % CHUNKS)
        if 0 <= k - 4 < units:
            stage_d((k - 4) // CHUNKS + 1, (k - 4) % CHUNKS)

    def finish(i):
        s = shard_at(i)

        @pl.when((s < z) & (z < planes - 1))
        def _():
            for n in range(CHUNKS + 1):
                z_up(s, n).wait_send()

        @pl.when((s > z) & (z > 0))
        def _():
            for n in range(CHUNKS + 1):
                z_dn(s, n).wait_send()

        for j in range(CHUNKS):
            x_copy(s, j).wait_send()
            y_copy(s, j).wait_send()
            if j > 0:
                d_copy(s, j).wait_send()
            for kind in range(4):
                m_copy(s, kind, j).wait_send()

    loads[0].wait()
    loads[1].wait()

    def head_of(ref, f, h):
        span = slice(h * HD, (h + 1) * HD)
        return jnp.concatenate([ref[f, row, span, :] for row in range(lat_rows)], axis=1)

    def state_step(f, carry):
        for h in range(groups * per):
            key = jnp.maximum(head_of(kv, f, h), jnp.zeros((), BF16))
            state = lax.dot_general(
                head_of(vv, f, h), key, (((1,), (1,)), ((), ())), preferred_element_type=F32
            )
            part[h // per, h % per, f] = state
            sent[h // per, h % per, f] = state.astype(BF16)
        return carry

    lax.fori_loop(0, frames, state_step, 0)

    mate_sums = [
        remote(sent.at[2 * chip + 1 - c], mate_in.at[chip], ps.at[chip], pr.at[chip], mate)
        for chip in range(groups // 2)
    ]
    for copy in mate_sums:
        copy.start()
    step(0)
    diagonal = (
        lax.broadcasted_iota(jnp.int32, (HD, HD), 0) == lax.broadcasted_iota(jnp.int32, (HD, HD), 1)
    ).astype(F32)
    for h in range(groups * per):
        span = slice(h * HD, (h + 1) * HD)
        gains[span, :] = jnp.sum(diagonal * gain_ref[:, span], axis=1, keepdims=True)
    for copy in mate_sums:
        copy.wait_recv()
    x_out[...] = (part[2 * (1 - x) + c] + mate_in[1 - x].astype(F32)).astype(BF16)
    x_sum = remote(x_out, x_in, qs, qr, xn)
    x_sum.start()
    own[...] = part[r] + mate_in[x].astype(F32)
    step(1)
    x_sum.wait_recv()

    @pl.when(z == 0)
    def _():
        chain_in[:, :, :HD, :] = jnp.zeros((per, 2, HD, HD), BF16)
        chain_in[:, :, HD:, :] = jnp.full((per, 2, chain_in.shape[2] - HD, HD), -1.0, BF16)

    def chain_copy(h):
        return remote(chain_out.at[h], chain_in.at[h], cs.at[h], cr.at[h], up)

    upper = z * 2 >= planes

    def early():
        step(2)
        step(3)

    pl.when(upper)(early)

    for h in range(per):

        @pl.when(z > 0)
        def _():
            pltpu.make_async_copy(chain_in.at[h], chain_in.at[h], cr.at[h]).wait()

        closed = chain_in[h, 0, :HD, :].astype(F32)
        opened = chain_in[h, 1, :HD, :].astype(F32)
        latest = chain_in[h, 0, HD:, :].astype(F32)[:1]
        for f in range(frames):
            summed = own[h, f] + x_in[h, f].astype(F32)
            flag = flag_ref[f].astype(F32)
            block = block_ref[f].astype(F32)
            advance = jnp.where(latest < block, 1.0, 0.0)
            select = jnp.maximum(advance, flag)
            reads[r, h, f] = (closed + select * opened + summed).astype(BF16)
            closed = closed + advance * opened
            opened = flag * summed + (1.0 - advance) * opened
            latest = jnp.maximum(latest, block)

        @pl.when(z < planes - 1)
        def _():
            chain_out[h, 0, :HD, :] = closed.astype(BF16)
            chain_out[h, 1, :HD, :] = opened.astype(BF16)
            chain_out[h, 0, HD:, :] = jnp.broadcast_to(
                latest, (chain_in.shape[2] - HD, HD)
            ).astype(BF16)
            chain_copy(h).start()

    other_x = 2 * (1 - x) + c
    read_mate = remote(reads.at[r], reads.at[r], gs.at[0], gr.at[0], mate)
    read_x = remote(reads.at[r], reads.at[r], gs.at[1], gr.at[1], xn)
    relay = remote(reads.at[other_x], reads.at[other_x], gs.at[2], gr.at[2], mate)
    read_x.start()
    read_mate.start()
    pl.when(jnp.logical_not(upper))(early)
    step(4)

    def got(group, sem):
        pltpu.make_async_copy(reads.at[group], reads.at[group], sem).wait()

    got(other_x, gr.at[1])
    relay.start()
    step(5)
    step(6)
    got(2 * x + 1 - c, gr.at[0])
    got(2 * (1 - x) + 1 - c, gr.at[2])
    loads[2].wait()

    def read_step(f, carry):
        for h in range(groups * per):
            query = jnp.maximum(head_of(qv, f, h), jnp.zeros((), BF16))
            attended = jnp.dot(
                reads[h // per, h % per, f], query, preferred_element_type=F32
            )
            mean = jnp.sum(attended * attended, axis=0, keepdims=True) * (1.0 / HD)
            value = attended * lax.rsqrt(mean + norm_eps) * gains[h * HD : (h + 1) * HD, :]
            at = h * HD % depth
            normed[h * HD // depth, at : at + HD, pl.ds(pl.multiple_of(f * tokens, tokens), tokens)] = (
                value.astype(BF16)
            )
        return carry

    lax.fori_loop(0, frames, read_step, 0)
    def product(s, lanes):
        return lax.dot_general(
            wv[s, :depth, lanes], normed[s], (((0,), (0,)), ((), ())), preferred_element_type=F32
        )

    def project(turn, lanes):
        s = z if turn == 0 else shard_at(turn)
        add = product(s, lanes)
        if turn > 0:
            add = acc[lanes, :] + add
        if turn < planes - 1:
            acc[lanes, :] = add
        else:
            for f in range(frames):
                for row in range(lat_rows):
                    at = (f * lat_rows + row) * lat_cols
                    out_ref[f, row, lanes, :] = add[:, at : at + lat_cols].astype(BF16)

    tile = 256

    def project_all(turn):
        def project_step(n, carry):
            project(turn, pl.ds(pl.multiple_of(n * tile, tile), tile))
            return carry

        lax.fori_loop(0, width // tile, project_step, 0)
        if width % tile:
            project(turn, slice(width // tile * tile, width))

    step(7)
    step(8)
    loads[3].wait()
    project_all(0)
    done = 8
    for turn in range(1, planes):
        last = turn * CHUNKS + 3 + (1 if turn < planes - 1 else 0)
        for k in range(done + 1, last + 1):
            step(k)
        done = max(done, last)
        stage_m(turn)
        project_all(turn)

    @pl.when(z < planes - 1)
    def _():
        for n in range(CHUNKS + 1):
            first_up(n).wait_send()
        for h in range(per):
            chain_copy(h).wait_send()

    @pl.when(z > 0)
    def _():
        for n in range(CHUNKS + 1):
            first_dn(n).wait_send()

    for i in range(1, planes):
        finish(i)
    for copy in mate_sums:
        copy.wait_send()
    x_sum.wait_send()
    read_mate.wait_send()
    read_x.wait_send()
    relay.wait_send()


def local_fused(mesh_shape, queries, keys, values, flags, blocks, out_weight, norm_gain):
    frames, lat_rows, lat_cols, width = queries.shape
    planes, groups = mesh_shape["frm"], mesh_shape["row"]
    per = HEADS // groups
    depth = out_weight.shape[0]
    rows, cols = round_up(depth, 64 * CHUNKS), round_up(width, 256)
    weight = jnp.pad(out_weight, ((0, rows - depth), (0, cols - width)))
    dma = pltpu.SemaphoreType.DMA
    shape = (frames, lat_rows, width, lat_cols)
    anywhere = pl.BlockSpec(memory_space=pl.ANY)
    scalar = pl.BlockSpec(memory_space=pltpu.SMEM)
    vector = pl.BlockSpec(memory_space=pltpu.VMEM)
    per_group = (per, frames, HD, HD)
    link = (per, 2, round_up(HD + 1, 16), HD)
    out = pl.pallas_call(
        functools.partial(fused, planes, "grp", "frm", "row"),
        out_shape=jax.ShapeDtypeStruct(shape, BF16),
        in_specs=[anywhere] * 4 + [vector, scalar, scalar],
        out_specs=vector,
        scratch_shapes=[
            pltpu.VMEM(shape, BF16),
            pltpu.VMEM(shape, BF16),
            pltpu.VMEM(shape, BF16),
            pltpu.VMEM((planes, rows, cols), BF16),
            pltpu.VMEM((groups,) + per_group, F32),
            pltpu.VMEM((groups,) + per_group, BF16),
            pltpu.VMEM((groups // 2,) + per_group, BF16),
            pltpu.VMEM(per_group, BF16),
            pltpu.VMEM(per_group, BF16),
            pltpu.VMEM(per_group, F32),
            pltpu.VMEM(link, BF16),
            pltpu.VMEM(link, BF16),
            pltpu.VMEM((groups,) + per_group, BF16),
            pltpu.VMEM((planes, depth, frames * lat_rows * lat_cols), BF16),
            pltpu.VMEM((width, 1), F32),
            pltpu.VMEM((width, frames * lat_rows * lat_cols), F32),
            dma((4,)),
        ]
        + [dma((planes, CHUNKS + 1))] * 3
        + [dma((planes, CHUNKS))] * 6
        + [dma((planes, 4 * CHUNKS))] * 2
        + [dma((groups // 2,))] * 2
        + [dma(()), dma(())]
        + [dma((per,))] * 2
        + [dma((3,))] * 2,
        compiler_params=pltpu.CompilerParams(
            collective_id=0, has_side_effects=True, vmem_limit_bytes=56 * 1024 * 1024
        ),
    )(
        *(jnp.swapaxes(a, 2, 3) for a in (queries, keys, values)), weight,
        norm_gain.reshape(1, width), flags, blocks,
    )
    return jnp.swapaxes(out, 2, 3)


def fits(mesh):
    grp, frm, row = mesh.shape["grp"], mesh.shape["frm"], mesh.shape["row"]
    return grp == 2 and row == 4 and frm > 2 and HEADS % row == 0 and HEADS % frm == 0


def solution(mesh):
    in_specs = (
        P(("grp", "frm"), "row", None, None),
        P(("grp", "frm"), "row", None, None),
        P(("grp", "frm"), "row", None, None),
        P(("grp", "frm")),
        P(("grp", "frm")),
        P("frm", None),
        P(),
    )
    out_specs = P(("grp", "frm"), "row", None, None)
    body = functools.partial(local_fused, dict(mesh.shape)) if fits(mesh) else local
    return jax.shard_map(body, mesh=mesh, in_specs=in_specs, out_specs=out_specs, check_vma=False)
```

```python
import functools

import jax
import jax.numpy as jnp
from jax import lax
from jax.sharding import PartitionSpec as P
from jax.experimental import pallas as pl
from jax.experimental.pallas import tpu as pltpu

HEADS = 20
HD = 112


norm_eps = 1e-06
CHUNKS = 3


def entering(part, axis, combine, identity):
    place = lax.axis_index(axis)
    gathered = jax.tree.map(lambda a: lax.all_gather(a, axis), part)
    state = jax.tree.map(lambda a, e: jnp.zeros_like(a) + jnp.asarray(e, a.dtype), part, identity)

    def one(step, state):
        return combine(
            state, jax.tree.map(lambda a: lax.dynamic_index_in_dim(a, step, 0, False), gathered)
        )

    return lax.fori_loop(0, place, one, state)


def combine(earlier, later):
    closed_a, opened_a, latest_a = earlier
    closed_b, opened_b, latest_b = later
    advance = (latest_a < latest_b).astype(jnp.float32)
    return (
        closed_a + closed_b + advance * opened_a,
        opened_b + (1.0 - advance) * opened_a,
        jnp.maximum(latest_a, latest_b),
    )


def empty_carry(length):
    return (
        jnp.zeros((length,), jnp.float32),
        jnp.zeros((length,), jnp.float32),
        jnp.full((1,), -1.0, jnp.float32),
    )


def frame_element(frame_states, flag_values, block_values, frame_idx):
    length = frame_states.shape[1]
    return (
        jnp.zeros((length,), jnp.float32),
        flag_values[frame_idx] * frame_states[frame_idx],
        block_values[frame_idx : frame_idx + 1],
    )


def fold_frames(frame_states, flag_values, block_values):
    running = empty_carry(frame_states.shape[1])
    for frame_idx in range(frame_states.shape[0]):
        running = combine(
            running, frame_element(frame_states, flag_values, block_values, frame_idx)
        )
    return running


def read_frames(prefix, frame_states, flag_values, block_values):
    running = prefix
    collected = []
    for frame_idx in range(frame_states.shape[0]):
        advance = (running[2] < block_values[frame_idx : frame_idx + 1]).astype(jnp.float32)
        select = jnp.maximum(advance, flag_values[frame_idx])
        collected.append(running[0] + select * running[1] + frame_states[frame_idx])
        running = combine(
            running, frame_element(frame_states, flag_values, block_values, frame_idx)
        )
    return jnp.stack(collected)


def local(queries, keys, values, flags, blocks, out_weight, norm_gain):
    frames, lat_rows, lat_cols, model_width = queries.shape
    tokens = lat_rows * lat_cols
    key_pos = jax.nn.relu(keys).reshape(frames, tokens, HEADS, HD)
    value_heads = values.reshape(frames, tokens, HEADS, HD)
    partial_value = jnp.einsum(
        "ftha,fthb->fhab", key_pos, value_heads, preferred_element_type=jnp.float32
    )
    partial_value = partial_value.reshape(frames, HEADS * HD * HD)
    flag_values = flags.astype(jnp.float32)
    block_values = blocks.astype(jnp.float32)
    summed = lax.psum(partial_value, "row")
    totals = fold_frames(summed, flag_values, block_values)
    prefix = entering(
        (totals[0], totals[1], totals[2]), "frm", combine, empty_carry(summed.shape[1])
    )
    read_states = read_frames(prefix, summed, flag_values, block_values)
    read_tensor = read_states.reshape(frames, HEADS, HD, HD)
    query_pos = jax.nn.relu(queries).reshape(frames, tokens, HEADS, HD).astype(jnp.float32)
    attended = jnp.einsum(
        "ftha,fhab->fthb", query_pos, read_tensor, precision=lax.Precision.HIGHEST
    )
    inv_rms = lax.rsqrt(jnp.mean(attended * attended, axis=-1, keepdims=True) + norm_eps)
    gain_table = norm_gain.reshape(HEADS, HD)
    normed = (
        (attended * inv_rms * gain_table).astype(jnp.bfloat16).reshape(frames * tokens, model_width)
    )
    projected = jnp.dot(
        normed,
        lax.all_gather(out_weight, "frm", axis=0, tiled=True),
        preferred_element_type=jnp.float32,
    )
    return projected.astype(jnp.bfloat16).reshape(frames, lat_rows, lat_cols, model_width)


MESH = pl.DeviceIdType.MESH
F32 = jnp.float32
BF16 = jnp.bfloat16


def round_up(size, unit):
    return (size + unit - 1) // unit * unit


def fused(
    planes, grp_axis, frm_axis, row_axis,
    q_hbm, k_hbm, v_hbm, w_hbm, gain_ref, flag_ref, block_ref, out_ref,
    qv, kv, vv, wl, wv, part, sent, mate_in, x_out, x_in, own, chain_in, chain_out, reads, normed, gains, acc,
    load_sem, zs_up, zs_dn, zr, xs, xr, ys, yr, ds, dr, ms, mr,
    ps, pr, qs, qr, cs, cr, gs, gr,
):
    g, z, r = lax.axis_index(grp_axis), lax.axis_index(frm_axis), lax.axis_index(row_axis)
    x, c = r // 2, r % 2
    mate = (g, z, 2 * x + 1 - c)
    xn = (g, z, 2 * (1 - x) + c)
    yn = (1 - g, z, r)
    up = (g, z + 1, r)
    dn = (g, z - 1, r)
    p_own, p_x, p_y, p_d = 2 * x + g, 2 * (1 - x) + g, 2 * x + 1 - g, 2 * (1 - x) + 1 - g
    frames, lat_rows, width, lat_cols = qv.shape
    tokens = lat_rows * lat_cols
    groups, per = part.shape[0], part.shape[1]
    rows, cols = wv.shape[1] // 4, wv.shape[2] // 2
    depth = normed.shape[1]

    chunk = rows // CHUNKS

    def cut(p, core, j):
        return (
            pl.ds(pl.multiple_of(p * rows + j * chunk, 16), chunk),
            pl.ds(pl.multiple_of(core * cols, 128), cols),
        )

    def piece(s, p, core, j):
        return wv.at[(s,) + cut(p, core, j)]

    def remote(src, dst, send, recv, to):
        return pltpu.make_async_remote_copy(
            src_ref=src, dst_ref=dst, send_sem=send, recv_sem=recv,
            device_id=to, device_id_type=MESH,
        )

    barrier = pltpu.get_barrier_semaphore()
    for other in (mate, xn, yn):
        pl.semaphore_signal(barrier, inc=1, device_id=other, device_id_type=MESH)

    @pl.when(z > 0)
    def _():
        pl.semaphore_signal(barrier, inc=1, device_id=dn, device_id_type=MESH)

    @pl.when(z < planes - 1)
    def _():
        pl.semaphore_signal(barrier, inc=1, device_id=up, device_id_type=MESH)

    loads = [
        pltpu.make_async_copy(k_hbm, kv, load_sem.at[0]),
        pltpu.make_async_copy(v_hbm, vv, load_sem.at[1]),
        pltpu.make_async_copy(q_hbm, qv, load_sem.at[2]),
        pltpu.make_async_copy(w_hbm, wl, load_sem.at[3]),
    ]
    for load in reversed(loads):
        load.start()
    loads[3].wait()
    wv[z, :depth, :width] = wl[...]
    inner = (z > 0) & (z < planes - 1)

    @pl.when(inner)
    def _():
        pl.semaphore_wait(barrier, 5)

    @pl.when(jnp.logical_not(inner))
    def _():
        pl.semaphore_wait(barrier, 4)

    along = [(p_own, j) for j in range(CHUNKS)] + [(p_d, 0)]

    def first_up(n):
        p, j = along[n]
        return remote(piece(z, p, c, j), piece(z, p, c, j), zs_up.at[z, n], zr.at[z, n], up)

    def first_dn(n):
        p, j = along[n]
        return remote(piece(z, p, c, j), piece(z, p, c, j), zs_dn.at[z, n], zr.at[z, n], dn)

    for n in range(CHUNKS + 1):

        @pl.when(z < planes - 1)
        def _():
            first_up(n).start()

        @pl.when(z > 0)
        def _():
            first_dn(n).start()

    def shard_at(i):
        near = jnp.minimum(z, planes - 1 - z)
        s = jnp.where(i - 1 >= near, i, i - 1)
        return jnp.where(z * 2 < planes, s, planes - 1 - s)

    def z_up(s, n):
        p, j = along[n]
        return remote(piece(s, p, c, j), piece(s, p, c, j), zs_up.at[s, n], zr.at[s, n], up)

    def z_dn(s, n):
        p, j = along[n]
        return remote(piece(s, p, c, j), piece(s, p, c, j), zs_dn.at[s, n], zr.at[s, n], dn)

    def x_copy(s, j):
        return remote(piece(s, p_own, c, j), piece(s, p_own, c, j), xs.at[s, j], xr.at[s, j], xn)

    def y_copy(s, j):
        return remote(piece(s, p_own, c, j), piece(s, p_own, c, j), ys.at[s, j], yr.at[s, j], yn)

    def d_copy(s, j):
        return remote(piece(s, p_x, c, j), piece(s, p_x, c, j), ds.at[s, j], dr.at[s, j], yn)

    def m_copy(s, kind, j):
        p = (p_own, p_x, p_y, p_d)[kind]
        at = kind * CHUNKS + j
        return remote(piece(s, p, c, j), piece(s, p, c, j), ms.at[s, at], mr.at[s, at], mate)

    def landed(s, p, core, j, sem):
        pltpu.make_async_copy(piece(s, p, core, j), piece(s, p, core, j), sem).wait()

    def stage_z(i, n):
        s = shard_at(i)
        p, j = along[n]
        landed(s, p, c, j, zr.at[s, n])

        @pl.when((s < z) & (z < planes - 1))
        def _():
            z_up(s, n).start()

        @pl.when((s > z) & (z > 0))
        def _():
            z_dn(s, n).start()

        if n < CHUNKS:
            y_copy(s, j).start()
            x_copy(s, j).start()
            m_copy(s, 0, j).start()
        else:
            m_copy(s, 3, j).start()

    def stage_xy(i, j):
        s = shard_at(i)
        landed(s, p_x, c, j, xr.at[s, j])
        if j > 0:
            d_copy(s, j).start()
        m_copy(s, 1, j).start()
        landed(s, p_y, c, j, yr.at[s, j])
        m_copy(s, 2, j).start()

    def stage_d(i, j):
        if j > 0:
            s = shard_at(i)
            landed(s, p_d, c, j, dr.at[s, j])
            m_copy(s, 3, j).start()

    def stage_m(i):
        s = shard_at(i)
        for kind, p in enumerate((p_own, p_x, p_y, p_d)):
            for j in range(CHUNKS):
                landed(s, p, 1 - c, j, mr.at[s, kind * CHUNKS + j])

    units = (planes - 1) * CHUNKS

    def step(k):
        if k < units:
            i, j = k // CHUNKS + 1, k % CHUNKS
            stage_z(i, j)
            if j == CHUNKS - 1:
                stage_z(i, CHUNKS)
        if 0 <= k - 3 < units:
            stage_xy((k - 3) // CHUNKS + 1, (k - 3) % CHUNKS)
        if 0 <= k - 6 < units:
            stage_d((k - 6) // CHUNKS + 1, (k - 6) % CHUNKS)

    def finish(i):
        s = shard_at(i)

        @pl.when((s < z) & (z < planes - 1))
        def _():
            for n in range(CHUNKS + 1):
                z_up(s, n).wait_send()

        @pl.when((s > z) & (z > 0))
        def _():
            for n in range(CHUNKS + 1):
                z_dn(s, n).wait_send()

        for j in range(CHUNKS):
            x_copy(s, j).wait_send()
            y_copy(s, j).wait_send()
            if j > 0:
                d_copy(s, j).wait_send()
            for kind in range(4):
                m_copy(s, kind, j).wait_send()

    loads[0].wait()
    loads[1].wait()

    def head_of(ref, f, h):
        span = slice(h * HD, (h + 1) * HD)
        return jnp.concatenate([ref[f, row, span, :] for row in range(lat_rows)], axis=1)

    def state_step(f, carry):
        for h in range(groups * per):
            key = jnp.maximum(head_of(kv, f, h), jnp.zeros((), BF16))
            state = lax.dot_general(
                head_of(vv, f, h), key, (((1,), (1,)), ((), ())), preferred_element_type=F32
            )
            part[h // per, h % per, f] = state
            sent[h // per, h % per, f] = state.astype(BF16)
        return carry

    lax.fori_loop(0, frames, state_step, 0)

    mate_sums = [
        remote(sent.at[2 * chip + 1 - c], mate_in.at[chip], ps.at[chip], pr.at[chip], mate)
        for chip in range(groups // 2)
    ]
    for copy in mate_sums:
        copy.start()
    step(0)
    diagonal = (
        lax.broadcasted_iota(jnp.int32, (HD, HD), 0) == lax.broadcasted_iota(jnp.int32, (HD, HD), 1)
    ).astype(F32)
    gain = gain_ref[...].reshape(1, width)
    for h in range(groups * per):
        span = slice(h * HD, (h + 1) * HD)
        gains[span, :] = jnp.sum(diagonal * gain[:, span], axis=1, keepdims=True)
    for copy in mate_sums:
        copy.wait_recv()
    x_out[...] = (part[2 * (1 - x) + c] + mate_in[1 - x].astype(F32)).astype(BF16)
    x_sum = remote(x_out, x_in, qs, qr, xn)
    x_sum.start()
    own[...] = part[r] + mate_in[x].astype(F32)
    step(1)
    x_sum.wait_recv()

    @pl.when(z == 0)
    def _():
        chain_in[:, :, :HD, :] = jnp.zeros((per, 2, HD, HD), BF16)
        chain_in[:, :, HD:, :] = jnp.full((per, 2, chain_in.shape[2] - HD, HD), -1.0, BF16)

    def chain_copy(h):
        return remote(chain_out.at[h], chain_in.at[h], cs.at[h], cr.at[h], up)

    upper = z * 2 >= planes

    def early():
        step(2)
        step(3)

    pl.when(upper)(early)

    for h in range(per):

        @pl.when(z > 0)
        def _():
            pltpu.make_async_copy(chain_in.at[h], chain_in.at[h], cr.at[h]).wait()

        closed = chain_in[h, 0, :HD, :].astype(F32)
        opened = chain_in[h, 1, :HD, :].astype(F32)
        latest = chain_in[h, 0, HD:, :].astype(F32)[:1]
        for f in range(frames):
            summed = own[h, f] + x_in[h, f].astype(F32)
            flag = flag_ref[f].astype(F32)
            block = block_ref[f].astype(F32)
            advance = jnp.where(latest < block, 1.0, 0.0)
            select = jnp.maximum(advance, flag)
            reads[r, h, f] = (closed + select * opened + summed).astype(BF16)
            closed = closed + advance * opened
            opened = flag * summed + (1.0 - advance) * opened
            latest = jnp.maximum(latest, block)

        @pl.when(z < planes - 1)
        def _():
            chain_out[h, 0, :HD, :] = closed.astype(BF16)
            chain_out[h, 1, :HD, :] = opened.astype(BF16)
            chain_out[h, 0, HD:, :] = jnp.broadcast_to(
                latest, (chain_in.shape[2] - HD, HD)
            ).astype(BF16)
            chain_copy(h).start()

    other_x = 2 * (1 - x) + c
    read_mate = remote(reads.at[r], reads.at[r], gs.at[0], gr.at[0], mate)
    read_x = remote(reads.at[r], reads.at[r], gs.at[1], gr.at[1], xn)
    relay = remote(reads.at[other_x], reads.at[other_x], gs.at[2], gr.at[2], mate)
    read_x.start()
    read_mate.start()
    pl.when(jnp.logical_not(upper))(early)
    step(4)

    def got(group, sem):
        pltpu.make_async_copy(reads.at[group], reads.at[group], sem).wait()

    got(other_x, gr.at[1])
    relay.start()
    step(5)
    step(6)
    got(2 * x + 1 - c, gr.at[0])
    got(2 * (1 - x) + 1 - c, gr.at[2])
    loads[2].wait()

    def read_step(f, carry):
        for h in range(groups * per):
            query = jnp.maximum(head_of(qv, f, h), jnp.zeros((), BF16))
            attended = jnp.dot(
                reads[h // per, h % per, f], query, preferred_element_type=F32
            )
            mean = jnp.sum(attended * attended, axis=0, keepdims=True) * (1.0 / HD)
            value = attended * lax.rsqrt(mean + norm_eps) * gains[h * HD : (h + 1) * HD, :]
            at = h * HD % depth
            normed[h * HD // depth, at : at + HD, pl.ds(pl.multiple_of(f * tokens, tokens), tokens)] = (
                value.astype(BF16)
            )
        return carry

    lax.fori_loop(0, frames, read_step, 0)
    def product(s, lanes):
        return lax.dot_general(
            wv[s, :depth, lanes], normed[s], (((0,), (0,)), ((), ())), preferred_element_type=F32
        )

    def project(turn, lanes):
        s = z if turn == 0 else shard_at(turn)
        add = product(s, lanes)
        if turn > 0:
            add = acc[lanes, :] + add
        if turn < planes - 1:
            acc[lanes, :] = add
        else:
            for f in range(frames):
                for row in range(lat_rows):
                    at = (f * lat_rows + row) * lat_cols
                    out_ref[f, row, lanes, :] = add[:, at : at + lat_cols].astype(BF16)

    tile = 256

    def project_all(turn):
        def project_step(n, carry):
            project(turn, pl.ds(pl.multiple_of(n * tile, tile), tile))
            return carry

        lax.fori_loop(0, width // tile, project_step, 0)
        if width % tile:
            project(turn, slice(width // tile * tile, width))

    step(7)
    step(8)
    project_all(0)
    done = 8
    for turn in range(1, planes):
        last = turn * CHUNKS + 5 + (1 if turn < planes - 1 else 0)
        for k in range(done + 1, last + 1):
            step(k)
        done = max(done, last)
        stage_m(turn)
        project_all(turn)

    @pl.when(z < planes - 1)
    def _():
        for n in range(CHUNKS + 1):
            first_up(n).wait_send()
        for h in range(per):
            chain_copy(h).wait_send()

    @pl.when(z > 0)
    def _():
        for n in range(CHUNKS + 1):
            first_dn(n).wait_send()

    for i in range(1, planes):
        finish(i)
    for copy in mate_sums:
        copy.wait_send()
    x_sum.wait_send()
    read_mate.wait_send()
    read_x.wait_send()
    relay.wait_send()


def local_fused(mesh_shape, queries, keys, values, flags, blocks, out_weight, norm_gain):
    frames, lat_rows, lat_cols, width = queries.shape
    planes, groups = mesh_shape["frm"], mesh_shape["row"]
    per = HEADS // groups
    depth = out_weight.shape[0]
    rows, cols = round_up(depth, 64 * CHUNKS), round_up(width, 256)
    dma = pltpu.SemaphoreType.DMA
    shape = (frames, lat_rows, width, lat_cols)
    anywhere = pl.BlockSpec(memory_space=pl.ANY)
    scalar = pl.BlockSpec(memory_space=pltpu.SMEM)
    vector = pl.BlockSpec(memory_space=pltpu.VMEM)
    per_group = (per, frames, HD, HD)
    link = (per, 2, round_up(HD + 1, 16), HD)
    out = pl.pallas_call(
        functools.partial(fused, planes, "grp", "frm", "row"),
        out_shape=jax.ShapeDtypeStruct(shape, BF16),
        in_specs=[anywhere] * 4 + [vector, scalar, scalar],
        out_specs=vector,
        scratch_shapes=[
            pltpu.VMEM(shape, BF16),
            pltpu.VMEM(shape, BF16),
            pltpu.VMEM(shape, BF16),
            pltpu.VMEM(out_weight.shape, BF16),
            pltpu.VMEM((planes, rows, cols), BF16),
            pltpu.VMEM((groups,) + per_group, F32),
            pltpu.VMEM((groups,) + per_group, BF16),
            pltpu.VMEM((groups // 2,) + per_group, BF16),
            pltpu.VMEM(per_group, BF16),
            pltpu.VMEM(per_group, BF16),
            pltpu.VMEM(per_group, F32),
            pltpu.VMEM(link, BF16),
            pltpu.VMEM(link, BF16),
            pltpu.VMEM((groups,) + per_group, BF16),
            pltpu.VMEM((planes, depth, frames * lat_rows * lat_cols), BF16),
            pltpu.VMEM((width, 1), F32),
            pltpu.VMEM((width, frames * lat_rows * lat_cols), F32),
            dma((4,)),
        ]
        + [dma((planes, CHUNKS + 1))] * 3
        + [dma((planes, CHUNKS))] * 6
        + [dma((planes, 4 * CHUNKS))] * 2
        + [dma((groups // 2,))] * 2
        + [dma(()), dma(())]
        + [dma((per,))] * 2
        + [dma((3,))] * 2,
        compiler_params=pltpu.CompilerParams(
            collective_id=0, has_side_effects=True, vmem_limit_bytes=56 * 1024 * 1024
        ),
    )(
        *(jnp.swapaxes(a, 2, 3) for a in (queries, keys, values)), out_weight,
        norm_gain, flags, blocks,
    )
    return jnp.swapaxes(out, 2, 3)


def fits(mesh):
    grp, frm, row = mesh.shape["grp"], mesh.shape["frm"], mesh.shape["row"]
    return grp == 2 and row == 4 and frm > 2 and HEADS % row == 0 and HEADS % frm == 0


def solution(mesh):
    in_specs = (
        P(("grp", "frm"), "row", None, None),
        P(("grp", "frm"), "row", None, None),
        P(("grp", "frm"), "row", None, None),
        P(("grp", "frm")),
        P(("grp", "frm")),
        P("frm", None),
        P(),
    )
    out_specs = P(("grp", "frm"), "row", None, None)
    body = functools.partial(local_fused, dict(mesh.shape)) if fits(mesh) else local
    return jax.shard_map(body, mesh=mesh, in_specs=in_specs, out_specs=out_specs, check_vma=False)
```

```python
import functools

import jax
import jax.numpy as jnp
from jax import lax
from jax.sharding import PartitionSpec as P
from jax.experimental import pallas as pl
from jax.experimental.pallas import tpu as pltpu

HEADS = 20
HD = 112


norm_eps = 1e-06
CHUNKS = 3


def entering(part, axis, combine, identity):
    place = lax.axis_index(axis)
    gathered = jax.tree.map(lambda a: lax.all_gather(a, axis), part)
    state = jax.tree.map(lambda a, e: jnp.zeros_like(a) + jnp.asarray(e, a.dtype), part, identity)

    def one(step, state):
        return combine(
            state, jax.tree.map(lambda a: lax.dynamic_index_in_dim(a, step, 0, False), gathered)
        )

    return lax.fori_loop(0, place, one, state)


def combine(earlier, later):
    closed_a, opened_a, latest_a = earlier
    closed_b, opened_b, latest_b = later
    advance = (latest_a < latest_b).astype(jnp.float32)
    return (
        closed_a + closed_b + advance * opened_a,
        opened_b + (1.0 - advance) * opened_a,
        jnp.maximum(latest_a, latest_b),
    )


def empty_carry(length):
    return (
        jnp.zeros((length,), jnp.float32),
        jnp.zeros((length,), jnp.float32),
        jnp.full((1,), -1.0, jnp.float32),
    )


def frame_element(frame_states, flag_values, block_values, frame_idx):
    length = frame_states.shape[1]
    return (
        jnp.zeros((length,), jnp.float32),
        flag_values[frame_idx] * frame_states[frame_idx],
        block_values[frame_idx : frame_idx + 1],
    )


def fold_frames(frame_states, flag_values, block_values):
    running = empty_carry(frame_states.shape[1])
    for frame_idx in range(frame_states.shape[0]):
        running = combine(
            running, frame_element(frame_states, flag_values, block_values, frame_idx)
        )
    return running


def read_frames(prefix, frame_states, flag_values, block_values):
    running = prefix
    collected = []
    for frame_idx in range(frame_states.shape[0]):
        advance = (running[2] < block_values[frame_idx : frame_idx + 1]).astype(jnp.float32)
        select = jnp.maximum(advance, flag_values[frame_idx])
        collected.append(running[0] + select * running[1] + frame_states[frame_idx])
        running = combine(
            running, frame_element(frame_states, flag_values, block_values, frame_idx)
        )
    return jnp.stack(collected)


def local(queries, keys, values, flags, blocks, out_weight, norm_gain):
    frames, lat_rows, lat_cols, model_width = queries.shape
    tokens = lat_rows * lat_cols
    key_pos = jax.nn.relu(keys).reshape(frames, tokens, HEADS, HD)
    value_heads = values.reshape(frames, tokens, HEADS, HD)
    partial_value = jnp.einsum(
        "ftha,fthb->fhab", key_pos, value_heads, preferred_element_type=jnp.float32
    )
    partial_value = partial_value.reshape(frames, HEADS * HD * HD)
    flag_values = flags.astype(jnp.float32)
    block_values = blocks.astype(jnp.float32)
    summed = lax.psum(partial_value, "row")
    totals = fold_frames(summed, flag_values, block_values)
    prefix = entering(
        (totals[0], totals[1], totals[2]), "frm", combine, empty_carry(summed.shape[1])
    )
    read_states = read_frames(prefix, summed, flag_values, block_values)
    read_tensor = read_states.reshape(frames, HEADS, HD, HD)
    query_pos = jax.nn.relu(queries).reshape(frames, tokens, HEADS, HD).astype(jnp.float32)
    attended = jnp.einsum(
        "ftha,fhab->fthb", query_pos, read_tensor, precision=lax.Precision.HIGHEST
    )
    inv_rms = lax.rsqrt(jnp.mean(attended * attended, axis=-1, keepdims=True) + norm_eps)
    gain_table = norm_gain.reshape(HEADS, HD)
    normed = (
        (attended * inv_rms * gain_table).astype(jnp.bfloat16).reshape(frames * tokens, model_width)
    )
    projected = jnp.dot(
        normed,
        lax.all_gather(out_weight, "frm", axis=0, tiled=True),
        preferred_element_type=jnp.float32,
    )
    return projected.astype(jnp.bfloat16).reshape(frames, lat_rows, lat_cols, model_width)


MESH = pl.DeviceIdType.MESH
F32 = jnp.float32
BF16 = jnp.bfloat16


def round_up(size, unit):
    return (size + unit - 1) // unit * unit


def fused(
    planes, grp_axis, frm_axis, row_axis,
    q_hbm, k_hbm, v_hbm, w_hbm, gain_ref, flag_ref, block_ref, out_ref,
    qv, kv, vv, wl, wv, part, sent, mate_in, x_out, x_in, own, chain_in, chain_out, reads, normed, gains, acc,
    load_sem, zs_up, zs_dn, zr, xs, xr, ys, yr, ds, dr, ms, mr,
    ps, pr, qs, qr, cs, cr, gs, gr,
):
    g, z, r = lax.axis_index(grp_axis), lax.axis_index(frm_axis), lax.axis_index(row_axis)
    x, c = r // 2, r % 2
    mate = (g, z, 2 * x + 1 - c)
    xn = (g, z, 2 * (1 - x) + c)
    yn = (1 - g, z, r)
    up = (g, z + 1, r)
    dn = (g, z - 1, r)
    p_own, p_x, p_y, p_d = 2 * x + g, 2 * (1 - x) + g, 2 * x + 1 - g, 2 * (1 - x) + 1 - g
    frames, lat_rows, width, lat_cols = qv.shape
    tokens = lat_rows * lat_cols
    groups, per = part.shape[0], part.shape[1]
    rows, cols = wv.shape[1] // 4, wv.shape[2] // 2
    depth = normed.shape[1]

    chunk = rows // CHUNKS

    def cut(p, core, j):
        return (
            pl.ds(pl.multiple_of(p * rows + j * chunk, 16), chunk),
            pl.ds(pl.multiple_of(core * cols, 128), cols),
        )

    def piece(s, p, core, j):
        return wv.at[(s,) + cut(p, core, j)]

    def remote(src, dst, send, recv, to):
        return pltpu.make_async_remote_copy(
            src_ref=src, dst_ref=dst, send_sem=send, recv_sem=recv,
            device_id=to, device_id_type=MESH,
        )

    barrier = pltpu.get_barrier_semaphore()
    for other in (mate, xn, yn):
        pl.semaphore_signal(barrier, inc=1, device_id=other, device_id_type=MESH)

    @pl.when(z > 0)
    def _():
        pl.semaphore_signal(barrier, inc=1, device_id=dn, device_id_type=MESH)

    @pl.when(z < planes - 1)
    def _():
        pl.semaphore_signal(barrier, inc=1, device_id=up, device_id_type=MESH)

    loads = [
        pltpu.make_async_copy(k_hbm, kv, load_sem.at[0]),
        pltpu.make_async_copy(v_hbm, vv, load_sem.at[1]),
        pltpu.make_async_copy(q_hbm, qv, load_sem.at[2]),
        pltpu.make_async_copy(w_hbm, wl, load_sem.at[3]),
    ]
    for load in reversed(loads):
        load.start()
    loads[3].wait()
    wv[z, :depth, :width] = wl[...]
    inner = (z > 0) & (z < planes - 1)

    @pl.when(inner)
    def _():
        pl.semaphore_wait(barrier, 5)

    @pl.when(jnp.logical_not(inner))
    def _():
        pl.semaphore_wait(barrier, 4)

    along = [(p_own, j) for j in range(CHUNKS)] + [(p_d, 0)]

    def first_up(n):
        p, j = along[n]
        return remote(piece(z, p, c, j), piece(z, p, c, j), zs_up.at[z, n], zr.at[z, n], up)

    def first_dn(n):
        p, j = along[n]
        return remote(piece(z, p, c, j), piece(z, p, c, j), zs_dn.at[z, n], zr.at[z, n], dn)

    for n in range(CHUNKS + 1):

        @pl.when(z < planes - 1)
        def _():
            first_up(n).start()

        @pl.when(z > 0)
        def _():
            first_dn(n).start()

    def shard_at(i):
        near = jnp.minimum(z, planes - 1 - z)
        s = jnp.where(i - 1 >= near, i, i - 1)
        return jnp.where(z * 2 < planes, s, planes - 1 - s)

    def z_up(s, n):
        p, j = along[n]
        return remote(piece(s, p, c, j), piece(s, p, c, j), zs_up.at[s, n], zr.at[s, n], up)

    def z_dn(s, n):
        p, j = along[n]
        return remote(piece(s, p, c, j), piece(s, p, c, j), zs_dn.at[s, n], zr.at[s, n], dn)

    def x_copy(s, j):
        return remote(piece(s, p_own, c, j), piece(s, p_own, c, j), xs.at[s, j], xr.at[s, j], xn)

    def y_copy(s, j):
        return remote(piece(s, p_own, c, j), piece(s, p_own, c, j), ys.at[s, j], yr.at[s, j], yn)

    def d_copy(s, j):
        return remote(piece(s, p_x, c, j), piece(s, p_x, c, j), ds.at[s, j], dr.at[s, j], yn)

    def m_copy(s, kind, j):
        p = (p_own, p_x, p_y, p_d)[kind]
        at = kind * CHUNKS + j
        return remote(piece(s, p, c, j), piece(s, p, c, j), ms.at[s, at], mr.at[s, at], mate)

    def landed(s, p, core, j, sem):
        pltpu.make_async_copy(piece(s, p, core, j), piece(s, p, core, j), sem).wait()

    def stage_z(i, n):
        s = shard_at(i)
        p, j = along[n]
        landed(s, p, c, j, zr.at[s, n])

        @pl.when((s < z) & (z < planes - 1))
        def _():
            z_up(s, n).start()

        @pl.when((s > z) & (z > 0))
        def _():
            z_dn(s, n).start()

        if n < CHUNKS:
            y_copy(s, j).start()
            x_copy(s, j).start()
            m_copy(s, 0, j).start()
        else:
            m_copy(s, 3, j).start()

    def stage_xy(i, j):
        s = shard_at(i)
        landed(s, p_x, c, j, xr.at[s, j])
        if j > 0:
            d_copy(s, j).start()
        m_copy(s, 1, j).start()
        landed(s, p_y, c, j, yr.at[s, j])
        m_copy(s, 2, j).start()

    def stage_d(i, j):
        if j > 0:
            s = shard_at(i)
            landed(s, p_d, c, j, dr.at[s, j])
            m_copy(s, 3, j).start()

    def stage_m(i):
        s = shard_at(i)
        for kind, p in enumerate((p_own, p_x, p_y, p_d)):
            for j in range(CHUNKS):
                landed(s, p, 1 - c, j, mr.at[s, kind * CHUNKS + j])

    units = (planes - 1) * CHUNKS

    def step(k):
        if k < units:
            i, j = k // CHUNKS + 1, k % CHUNKS
            stage_z(i, j)
            if j == CHUNKS - 1:
                stage_z(i, CHUNKS)
        if 0 <= k - 3 < units:
            stage_xy((k - 3) // CHUNKS + 1, (k - 3) % CHUNKS)
        if 0 <= k - 6 < units:
            stage_d((k - 6) // CHUNKS + 1, (k - 6) % CHUNKS)

    def finish(i):
        s = shard_at(i)

        @pl.when((s < z) & (z < planes - 1))
        def _():
            for n in range(CHUNKS + 1):
                z_up(s, n).wait_send()

        @pl.when((s > z) & (z > 0))
        def _():
            for n in range(CHUNKS + 1):
                z_dn(s, n).wait_send()

        for j in range(CHUNKS):
            x_copy(s, j).wait_send()
            y_copy(s, j).wait_send()
            if j > 0:
                d_copy(s, j).wait_send()
            for kind in range(4):
                m_copy(s, kind, j).wait_send()

    loads[0].wait()
    loads[1].wait()

    def head_of(ref, f, h):
        span = slice(h * HD, (h + 1) * HD)
        return jnp.concatenate([ref[f, row, span, :] for row in range(lat_rows)], axis=1)

    def state_step(f, carry):
        for h in range(groups * per):
            key = jnp.maximum(head_of(kv, f, h), jnp.zeros((), BF16))
            state = lax.dot_general(
                head_of(vv, f, h), key, (((1,), (1,)), ((), ())), preferred_element_type=F32
            )
            part[h // per, h % per, f] = state
            sent[h // per, h % per, f] = state.astype(BF16)
        return carry

    lax.fori_loop(0, frames, state_step, 0)

    mate_sums = [
        remote(sent.at[2 * chip + 1 - c], mate_in.at[chip], ps.at[chip], pr.at[chip], mate)
        for chip in range(groups // 2)
    ]
    for copy in mate_sums:
        copy.start()
    step(0)
    diagonal = (
        lax.broadcasted_iota(jnp.int32, (HD, HD), 0) == lax.broadcasted_iota(jnp.int32, (HD, HD), 1)
    ).astype(F32)
    gain = gain_ref[...].reshape(1, width)
    for h in range(groups * per):
        span = slice(h * HD, (h + 1) * HD)
        gains[span, :] = jnp.sum(diagonal * gain[:, span], axis=1, keepdims=True)
    for copy in mate_sums:
        copy.wait_recv()
    x_out[...] = (part[2 * (1 - x) + c] + mate_in[1 - x].astype(F32)).astype(BF16)
    x_sum = remote(x_out, x_in, qs, qr, xn)
    x_sum.start()
    own[...] = part[r] + mate_in[x].astype(F32)
    step(1)
    x_sum.wait_recv()

    @pl.when(z == 0)
    def _():
        chain_in[:, :, :HD, :] = jnp.zeros((per, 2, HD, HD), BF16)
        chain_in[:, :, HD:, :] = jnp.full((per, 2, chain_in.shape[2] - HD, HD), -1.0, BF16)

    def chain_copy(h):
        return remote(chain_out.at[h], chain_in.at[h], cs.at[h], cr.at[h], up)

    upper = z * 2 >= planes

    def early():
        step(2)
        step(3)

    pl.when(upper)(early)

    for h in range(per):

        @pl.when(z > 0)
        def _():
            pltpu.make_async_copy(chain_in.at[h], chain_in.at[h], cr.at[h]).wait()

        closed = chain_in[h, 0, :HD, :].astype(F32)
        opened = chain_in[h, 1, :HD, :].astype(F32)
        latest = chain_in[h, 0, HD:, :].astype(F32)[:1]
        for f in range(frames):
            summed = own[h, f] + x_in[h, f].astype(F32)
            flag = flag_ref[f].astype(F32)
            block = block_ref[f].astype(F32)
            advance = jnp.where(latest < block, 1.0, 0.0)
            select = jnp.maximum(advance, flag)
            reads[r, h, f] = (closed + select * opened + summed).astype(BF16)
            closed = closed + advance * opened
            opened = flag * summed + (1.0 - advance) * opened
            latest = jnp.maximum(latest, block)

        @pl.when(z < planes - 1)
        def _():
            chain_out[h, 0, :HD, :] = closed.astype(BF16)
            chain_out[h, 1, :HD, :] = opened.astype(BF16)
            chain_out[h, 0, HD:, :] = jnp.broadcast_to(
                latest, (chain_in.shape[2] - HD, HD)
            ).astype(BF16)
            chain_copy(h).start()

    other_x = 2 * (1 - x) + c
    read_mate = remote(reads.at[r], reads.at[r], gs.at[0], gr.at[0], mate)
    read_x = remote(reads.at[r], reads.at[r], gs.at[1], gr.at[1], xn)
    relay = remote(reads.at[other_x], reads.at[other_x], gs.at[2], gr.at[2], mate)
    read_x.start()
    read_mate.start()
    pl.when(jnp.logical_not(upper))(early)
    step(4)

    def got(group, sem):
        pltpu.make_async_copy(reads.at[group], reads.at[group], sem).wait()

    got(other_x, gr.at[1])
    relay.start()
    step(5)
    step(6)
    got(2 * x + 1 - c, gr.at[0])
    got(2 * (1 - x) + 1 - c, gr.at[2])
    loads[2].wait()

    def read_step(f, carry):
        for h in range(groups * per):
            query = jnp.maximum(head_of(qv, f, h), jnp.zeros((), BF16))
            attended = jnp.dot(
                reads[h // per, h % per, f], query, preferred_element_type=F32
            )
            mean = jnp.sum(attended * attended, axis=0, keepdims=True) * (1.0 / HD)
            value = attended * lax.rsqrt(mean + norm_eps) * gains[h * HD : (h + 1) * HD, :]
            at = h * HD % depth
            normed[h * HD // depth, at : at + HD, pl.ds(pl.multiple_of(f * tokens, tokens), tokens)] = (
                value.astype(BF16)
            )
        return carry

    lax.fori_loop(0, frames, read_step, 0)
    def product(s, lanes):
        return lax.dot_general(
            wv[s, :depth, lanes], normed[s], (((0,), (0,)), ((), ())), preferred_element_type=F32
        )

    def project(turn, lanes):
        s = z if turn == 0 else shard_at(turn)
        add = product(s, lanes)
        if turn > 0:
            add = acc[lanes, :] + add
        if turn < planes - 1:
            acc[lanes, :] = add
        else:
            for f in range(frames):
                for row in range(lat_rows):
                    at = (f * lat_rows + row) * lat_cols
                    out_ref[f, row, lanes, :] = add[:, at : at + lat_cols].astype(BF16)

    tile = 256

    def project_all(turn):
        def project_step(n, carry):
            project(turn, pl.ds(pl.multiple_of(n * tile, tile), tile))
            return carry

        lax.fori_loop(0, width // tile, project_step, 0)
        if width % tile:
            project(turn, slice(width // tile * tile, width))

    step(7)
    step(8)
    project_all(0)
    done = 8
    for turn in range(1, planes):
        last = turn * CHUNKS + 5 + (1 if turn < planes - 1 else 0)
        last = max(last, units + 2)
        for k in range(done + 1, last + 1):
            step(k)
        done = max(done, last)
        stage_m(turn)
        project_all(turn)

    @pl.when(z < planes - 1)
    def _():
        for n in range(CHUNKS + 1):
            first_up(n).wait_send()
        for h in range(per):
            chain_copy(h).wait_send()

    @pl.when(z > 0)
    def _():
        for n in range(CHUNKS + 1):
            first_dn(n).wait_send()

    for i in range(1, planes):
        finish(i)
    for copy in mate_sums:
        copy.wait_send()
    x_sum.wait_send()
    read_mate.wait_send()
    read_x.wait_send()
    relay.wait_send()


def local_fused(mesh_shape, queries, keys, values, flags, blocks, out_weight, norm_gain):
    frames, lat_rows, lat_cols, width = queries.shape
    planes, groups = mesh_shape["frm"], mesh_shape["row"]
    per = HEADS // groups
    depth = out_weight.shape[0]
    rows, cols = round_up(depth, 64 * CHUNKS), round_up(width, 256)
    dma = pltpu.SemaphoreType.DMA
    shape = (frames, lat_rows, width, lat_cols)
    anywhere = pl.BlockSpec(memory_space=pl.ANY)
    scalar = pl.BlockSpec(memory_space=pltpu.SMEM)
    vector = pl.BlockSpec(memory_space=pltpu.VMEM)
    per_group = (per, frames, HD, HD)
    link = (per, 2, round_up(HD + 1, 16), HD)
    out = pl.pallas_call(
        functools.partial(fused, planes, "grp", "frm", "row"),
        out_shape=jax.ShapeDtypeStruct(shape, BF16),
        in_specs=[anywhere] * 4 + [vector, scalar, scalar],
        out_specs=vector,
        scratch_shapes=[
            pltpu.VMEM(shape, BF16),
            pltpu.VMEM(shape, BF16),
            pltpu.VMEM(shape, BF16),
            pltpu.VMEM(out_weight.shape, BF16),
            pltpu.VMEM((planes, rows, cols), BF16),
            pltpu.VMEM((groups,) + per_group, F32),
            pltpu.VMEM((groups,) + per_group, BF16),
            pltpu.VMEM((groups // 2,) + per_group, BF16),
            pltpu.VMEM(per_group, BF16),
            pltpu.VMEM(per_group, BF16),
            pltpu.VMEM(per_group, F32),
            pltpu.VMEM(link, BF16),
            pltpu.VMEM(link, BF16),
            pltpu.VMEM((groups,) + per_group, BF16),
            pltpu.VMEM((planes, depth, frames * lat_rows * lat_cols), BF16),
            pltpu.VMEM((width, 1), F32),
            pltpu.VMEM((width, frames * lat_rows * lat_cols), F32),
            dma((4,)),
        ]
        + [dma((planes, CHUNKS + 1))] * 3
        + [dma((planes, CHUNKS))] * 6
        + [dma((planes, 4 * CHUNKS))] * 2
        + [dma((groups // 2,))] * 2
        + [dma(()), dma(())]
        + [dma((per,))] * 2
        + [dma((3,))] * 2,
        compiler_params=pltpu.CompilerParams(
            collective_id=0, has_side_effects=True, vmem_limit_bytes=56 * 1024 * 1024
        ),
    )(
        *(jnp.swapaxes(a, 2, 3) for a in (queries, keys, values)), out_weight,
        norm_gain, flags, blocks,
    )
    return jnp.swapaxes(out, 2, 3)


def fits(mesh):
    grp, frm, row = mesh.shape["grp"], mesh.shape["frm"], mesh.shape["row"]
    return grp == 2 and row == 4 and frm > 2 and HEADS % row == 0 and HEADS % frm == 0


def solution(mesh):
    in_specs = (
        P(("grp", "frm"), "row", None, None),
        P(("grp", "frm"), "row", None, None),
        P(("grp", "frm"), "row", None, None),
        P(("grp", "frm")),
        P(("grp", "frm")),
        P("frm", None),
        P(),
    )
    out_specs = P(("grp", "frm"), "row", None, None)
    body = functools.partial(local_fused, dict(mesh.shape)) if fits(mesh) else local
    return jax.shard_map(body, mesh=mesh, in_specs=in_specs, out_specs=out_specs, check_vma=False)
```
